128 devices in a mesh: gx: 8 (over z, x_hi), gy: 4 (over x_lo, core), gz: 4 (over y).
Axes of the slice: x: 4 (x_hi: 2, x_lo: 2; x = x_hi * 2 + x_lo), y: 4, z: 4, core: 2. Of those that a mesh axis runs over, the one named last changes fastest.
Arguments:
- fixed_image: bfloat16 [256, 512, 1024], P('gz', 'gy', 'gx'), may hold values from -6 to 6
- moving_image: bfloat16 [256, 512, 1024], P('gz', 'gy', 'gx'), may hold values from -6 to 6
- block_shift: int32 [2, 4, 4, 8], P(None, 'gz', 'gy', 'gx'), may hold values from -1 to 0
- fraction: int32 [3, 4, 4, 8], P(None, 'gz', 'gy', 'gx'), may hold values from 0 to 63
- brick_valid: int32 [4, 4, 8], P('gz', 'gy', 'gx'), may hold values 0 or 1
- precond_x: float32 [64, 64], replicated, may hold values from -0.75 to 0.75
- precond_y: float32 [32, 32], replicated, may hold values from -1 to 1
- precond_z: float32 [16, 16], replicated, may hold values from -1.5 to 1.5
Outputs:
- gradient: float32 [3, 32, 64, 128], P(None, 'gz', 'gy', 'gx')
The draws below stay inside these ranges and needn't reach their ends.
All inputs are finite; a program needn't handle non-finite values. No bound on the sum of `brick_valid` on one device may be relied on, other than what follows from the above.
Results may differ from the reference program's by a relative error of at most 0.00035.
Values may be sent and summed in bfloat16 or wider, within the bound.
A program may use at most 192 MiB of HBM per device.

```python
import jax
import jax.numpy as jnp
from jax import lax

BXY = 128
BZ = 64
S = 8
NBX = 8
NBY = 4
NBZ = 4
NX = 1024
NY = 512
NZ = 256
CNX = 128
CNY = 64
CNZ = 32
CCX = 64
CCY = 32
CCZ = 16


def touch_ends(drawn, own_key, low, high):
    extent = drawn.shape
    spot = [jax.random.randint(jax.random.fold_in(own_key, axis), (), 0, extent[axis]) for axis in range(len(extent))]
    drawn = drawn.at[tuple(spot)].set(low)
    longest = extent.index(max(extent))
    spot[longest] = (spot[longest] + 1) % extent[longest]
    return drawn.at[tuple(spot)].set(high)


def level_of(stream_key, extent, split, low, largest):
    loudness = 1.0
    for position, shards_of in split:
        draws = jax.random.uniform(jax.random.fold_in(jax.random.fold_in(stream_key, 6), position), (shards_of,), jnp.float32, low / len(split), largest / len(split))
        loudness = loudness * jnp.repeat(jnp.exp(draws), extent[position] // shards_of).reshape((-1,) + (1,) * (len(extent) - 1 - position))
    return loudness


def gaussian(stream_key, shape, spread, most, shards=(), kind=jnp.bfloat16):
    loudness = level_of(stream_key, shape, shards, -0.22, 0.18) if shards else 1.0
    values = jax.random.normal(stream_key, shape, jnp.float32) * spread * loudness
    return jnp.minimum(jnp.maximum(values, -most), most).astype(kind)


def setup_inputs(seed: int = 0) -> dict:
    keys = jax.random.split(jax.random.key(seed), 9)
    return {
        "fixed_image": gaussian(keys[0], (NZ, NY, NX), 1.0, 6.0, ((0, 4), (1, 4), (2, 8))),
        "moving_image": gaussian(keys[1], (NZ, NY, NX), 1.0, 6.0, ((0, 4), (1, 4), (2, 8))),
        "block_shift": touch_ends(jax.random.randint(keys[2], (2, NBZ, NBY, NBX), -1, 1), jax.random.fold_in(keys[2], 1), -1, 0).astype(jnp.int32),
        "fraction": touch_ends(jax.random.randint(keys[3], (3, NBZ, NBY, NBX), 0, 64), jax.random.fold_in(keys[3], 1), 0, 63).astype(jnp.int32),
        "brick_valid": touch_ends((jax.random.randint(keys[4], (NBZ, NBY, NBX), 0, 8) < 7).astype(jnp.int32), jax.random.fold_in(keys[4], 1), 0, 1),
        "precond_x": gaussian(keys[5], (CCX, CCX), CCX ** -0.5, 0.75, (), jnp.float32),
        "precond_y": gaussian(keys[6], (CCY, CCY), CCY ** -0.5, 1.0, (), jnp.float32),
        "precond_z": gaussian(keys[7], (CCZ, CCZ), CCZ ** -0.5, 1.5, (), jnp.float32),
    }


HIGH = lax.Precision.HIGHEST


def lerp(values, weight, axis):
    size = values.shape[axis]
    lower = lax.slice_in_dim(values, 0, size - 1, axis=axis)
    upper = lax.slice_in_dim(values, 1, size, axis=axis)
    return (1.0 - weight) * lower + weight * upper


def differ(values, axis):
    size = values.shape[axis]
    return lax.slice_in_dim(values, 1, size, axis=axis) - lax.slice_in_dim(values, 0, size - 1, axis=axis)


def brick_force(slab, fixed, weights, valid):
    samples = slab.astype(jnp.float32)
    along_x = lerp(samples, weights[0], 2)
    diff_x = differ(samples, 2)
    along_xy = lerp(along_x, weights[1], 1)
    diff_xy = lerp(diff_x, weights[1], 1)
    diff_yx = differ(along_x, 1)
    warped = lerp(along_xy, weights[2], 0)
    grad_x = lerp(diff_xy, weights[2], 0)
    grad_y = lerp(diff_yx, weights[2], 0)
    grad_z = differ(along_xy, 0)
    resid = valid * (warped - fixed.astype(jnp.float32))
    return jnp.stack([resid * grad_x, resid * grad_y, resid * grad_z])


def spline_basis(vox_start, vox_count, pt_start, pt_count, spacing):
    place = (vox_start + jnp.arange(vox_count, dtype=jnp.int32)).astype(jnp.float32)
    point = (pt_start + jnp.arange(pt_count, dtype=jnp.int32)).astype(jnp.float32)
    dist = jnp.abs(place[:, None] - spacing * point[None, :]) / spacing
    inner = 2.0 / 3.0 - dist * dist + dist * dist * dist / 2.0
    outer = (2.0 - dist) ** 3 / 6.0
    return jnp.where(dist < 1.0, inner, jnp.where(dist < 2.0, outer, 0.0)).astype(jnp.float32)


def contract(field, basis_x, basis_y, basis_z):
    temp = jnp.einsum("dzyx,xp->dzyp", field, basis_x, precision=HIGH)
    temp = jnp.einsum("dzyp,yq->dzqp", temp, basis_y, precision=HIGH)
    return jnp.einsum("dzqp,zr->drqp", temp, basis_z, precision=HIGH)


def restrict(coarse_count, fine_start, fine_count):
    coarse_idx = jnp.arange(coarse_count, dtype=jnp.int32)[:, None]
    fine_idx = fine_start + jnp.arange(fine_count, dtype=jnp.int32)[None, :]
    gap = jnp.abs(fine_idx - 2 * coarse_idx)
    return jnp.where(gap == 0, 0.75, jnp.where(gap == 1, 0.5, jnp.where(gap == 2, 0.125, 0.0))).astype(jnp.float32)


def reference(fixed_image, moving_image, block_shift, fraction, brick_valid, precond_x, precond_y, precond_z):
    padded = jnp.pad(moving_image, ((0, 1), (BXY, 1), (BXY, 1)))

    def one_brick(index):
        lay = index // (NBY * NBX)
        row = (index // NBX) % NBY
        col = index % NBX
        start_x = (col * BXY + BXY + BXY * block_shift[0, lay, row, col]).astype(jnp.int32)
        start_y = (row * BXY + BXY + BXY * block_shift[1, lay, row, col]).astype(jnp.int32)
        start_z = (lay * BZ).astype(jnp.int32)
        slab = lax.dynamic_slice(padded, (start_z, start_y, start_x), (BZ + 1, BXY + 1, BXY + 1))
        fixed = lax.dynamic_slice(fixed_image, (start_z, (row * BXY).astype(jnp.int32), (col * BXY).astype(jnp.int32)), (BZ, BXY, BXY))
        weights = fraction[:, lay, row, col].astype(jnp.float32) / 64.0
        valid = brick_valid[lay, row, col].astype(jnp.float32)
        return brick_force(slab, fixed, weights, valid)

    forces = lax.map(one_brick, jnp.arange(NBX * NBY * NBZ, dtype=jnp.int32))
    forces = forces.reshape(NBZ, NBY, NBX, 3, BZ, BXY, BXY).transpose(3, 0, 4, 1, 5, 2, 6).reshape(3, NZ, NY, NX)
    fine = contract(forces, spline_basis(0, NX, 0, CNX, S), spline_basis(0, NY, 0, CNY, S), spline_basis(0, NZ, 0, CNZ, S)) * (S ** -1.5)
    restrict_x = restrict(CCX, 0, CNX)
    restrict_y = restrict(CCY, 0, CNY)
    restrict_z = restrict(CCZ, 0, CNZ)
    coarse = jnp.einsum("drqp,kr->dkqp", fine, restrict_z, precision=HIGH)
    coarse = jnp.einsum("dkqp,jq->dkjp", coarse, restrict_y, precision=HIGH)
    coarse = jnp.einsum("dkjp,ip->dkji", coarse, restrict_x, precision=HIGH)
    corrected = jnp.einsum("dkji,ai->dkja", coarse, precond_x, precision=HIGH)
    corrected = jnp.einsum("dkja,bj->dkba", corrected, precond_y, precision=HIGH)
    corrected = jnp.einsum("dkba,ck->dcba", corrected, precond_z, precision=HIGH)
    back = jnp.einsum("dkji,kr->drji", corrected, restrict_z, precision=HIGH)
    back = jnp.einsum("drji,jq->drqi", back, restrict_y, precision=HIGH)
    back = jnp.einsum("drqi,ip->drqp", back, restrict_x, precision=HIGH)
    return fine + back
```

```python
import functools

import jax
import jax.numpy as jnp
import numpy as np
from jax import lax
from jax.experimental import pallas as pl
from jax.experimental.pallas import tpu as pltpu
from jax.sharding import PartitionSpec as P

S = 8
SIDE = 128
DEPTH = 64
CELLS = DEPTH // S
GX, GY, GZ = 8, 4, 4
FULL = lax.Precision.HIGHEST
F32 = jnp.float32
BF16 = jnp.bfloat16
MESH = pl.DeviceIdType.MESH


def tap_polynomials():
    j = np.arange(S, dtype=np.float64)
    basis = np.stack(
        [np.ones(S), j + 1, (j + 1) * (j + 2) / 2, (j + 1) * (j + 2) * (j + 3) / 6], axis=1
    )
    taps = []
    for a in range(4):
        u = np.abs(j / S - (a - 1))
        taps.append(
            np.where(u < 1, 2 / 3 - u**2 + u**3 / 2, np.where(u < 2, (2 - u) ** 3 / 6, 0.0))
        )
    return np.linalg.lstsq(basis, np.stack(taps, axis=1), rcond=None)[0]


TAPS = tap_polynomials()


def iota(shape, dim):
    return lax.broadcasted_iota(jnp.int32, shape, dim)


def spline(distance):
    dist = jnp.abs(distance)
    inner = 2.0 / 3.0 - dist * dist + dist * dist * dist / 2.0
    far = 2.0 - dist
    outer = far * far * far / 6.0
    return jnp.where(dist < 1.0, inner, jnp.where(dist < 2.0, outer, 0.0))


def weight(gap):
    gap = jnp.abs(gap)
    return jnp.where(gap == 0, 0.75, jnp.where(gap == 1, 0.5, jnp.where(gap == 2, 0.125, 0.0)))


def split(value):
    high = value.astype(BF16)
    return high, (value - high.astype(F32)).astype(BF16)


def mm(a, b):
    return jnp.dot(a, b, preferred_element_type=F32)


def mm_full(a, b, dims=((1,), (0,))):
    return lax.dot_general(a, b, (dims, ((), ())), precision=FULL, preferred_element_type=F32)


def kernel(
    mov, fix, shift, frac, valid, px, py, pz, out,
    own, relay, land, stage, sib1, sib2, sib3, fixed,
    flag_out, flag_in, t_buf, s_buf, k_buf, t_sel, a_bot, b_bot,
    lhs, rhs, a_buf, b_buf, mom, rhs_x, lhs_y, acc, w_c,
    w_z, w_x, m_y, c_z, c_y, c_x, f_z, f_y, f_x, fold, h_x,
    local_sem, h1_s, h1_r, h2_s, h2_r, s1_s, s1_r, s2_s, s2_r, s3_s, s3_r,
    edge_s, edge_r, fine_s, fine_r, cz_s, cz_r, cy_s, cy_r, cx_s, cx_r,
):
    g, r, l = lax.axis_index("gx"), lax.axis_index("gy"), lax.axis_index("gz")
    across = lax.rem(r + 2, GY)
    sibling = (g, r + 1 - 2 * lax.rem(r, 2), l)
    partner = (g, across, l)

    def remote(src, dst, send, recv, device):
        return pltpu.make_async_remote_copy(
            src_ref=src, dst_ref=dst, send_sem=send, recv_sem=recv,
            device_id=device, device_id_type=MESH,
        )

    load_own = pltpu.make_async_copy(mov, own.at[pl.ds(0, DEPTH)], local_sem.at[0])
    load_fixed = pltpu.make_async_copy(fix, fixed, local_sem.at[1])
    load_own.start()
    load_fixed.start()

    oy = shift[1, 0, 0, 0]
    ox = shift[0, 0, 0, 0]
    tx = frac[0, 0, 0, 0].astype(F32) / 64.0
    ty = frac[1, 0, 0, 0].astype(F32) / 64.0
    tz = frac[2, 0, 0, 0].astype(F32) / 64.0
    live = valid[0, 0, 0].astype(F32)

    flag_out[...] = jnp.full((SIDE, SIDE), -oy.astype(F32), F32).astype(BF16)

    peers = [(lax.rem(g + o, GX), r, l) for o in range(1, GX)]
    peers += [(g, lax.rem(r + o, GY), l) for o in range(1, GY)]
    peers += [(g, r, lax.rem(l + o, GZ)) for o in range(1, GZ)]
    peers += [
        (lax.rem(g + dx, GX), lax.rem(r + dy, GY), l) for dx in (1, GX - 1) for dy in (1, 2, 3)
    ]
    barrier = pltpu.get_barrier_semaphore()
    for peer in peers:
        pl.semaphore_signal(barrier, inc=1, device_id=peer, device_id_type=MESH)
    pl.semaphore_wait(barrier, len(peers))

    def cell_planes(k):
        return pl.ds(pl.multiple_of(k * S, S), S)

    last = pl.ds(DEPTH, 1)

    def h1(sl, i):
        src = own if sl is last else mov
        return remote(
            src.at[sl], relay.at[sl], h1_s.at[i], h1_r.at[i], (lax.rem(g + 1, GX), across, l)
        )

    def h2(src, sl, i):
        return remote(src.at[sl], land.at[sl], h2_s.at[i], h2_r.at[i], partner)

    def s2(sl, i):
        return remote(relay.at[sl], sib2.at[sl], s2_s.at[i], s2_r.at[i], sibling)

    def s3(sl, i):
        return remote(land.at[sl], sib3.at[sl], s3_s.at[i], s3_r.at[i], sibling)

    has_next, has_prev = g < GX - 1, g > 0
    above, below = l < GZ - 1, l > 0

    plane = remote(mov.at[pl.ds(0, 1)], own.at[last], edge_s.at[8], edge_r.at[8], (g, r, lax.rem(l + GZ - 1, GZ)))
    flag = remote(flag_out, flag_in, edge_s.at[9], edge_r.at[9], partner)
    s1_bulk = remote(mov, sib1.at[pl.ds(0, DEPTH)], s1_s.at[0], s1_r.at[0], sibling)
    s1_last = remote(own.at[last], sib1.at[last], s1_s.at[1], s1_r.at[1], sibling)

    @pl.when(below)
    def _():
        plane.start()

    flag.start()

    @pl.when(has_next)
    def _():
        h1(cell_planes(7), 7).start()
        h1(cell_planes(6), 6).start()

    s1_bulk.start()

    zero_plane = jnp.zeros((1, SIDE, SIDE), BF16)

    @pl.when(jnp.logical_not(above))
    def _():
        own[pl.ds(DEPTH, 1)] = zero_plane

    @pl.when(jnp.logical_not(has_prev))
    def _():
        def clear(z, carry):
            relay[pl.ds(z, 1)] = zero_plane
            return carry

        lax.fori_loop(0, DEPTH + 1, clear, 0)

    load_own.wait()
    lane = iota((SIDE, SIDE), 1)
    row = iota((SIDE, SIDE), 0)

    def edge_step(z, carry):
        t, s = carry
        value = own[z].astype(F32)
        t = jnp.where(lane == z, jnp.broadcast_to(value[:, 0:1], (SIDE, SIDE)), t)
        s = jnp.where(row[:80] == z, jnp.broadcast_to(value[0:1, :], (80, SIDE)), s)
        return t, s

    t_own, s_own = lax.fori_loop(
        0, DEPTH, edge_step, (jnp.zeros((SIDE, SIDE), F32), jnp.zeros((80, SIDE), F32))
    )

    @pl.when(above)
    def _():
        plane.wait_recv()

    t_own, s_own = edge_step(DEPTH, (t_own, s_own))
    t_buf[0] = t_own.astype(BF16)
    s_buf[0] = s_own.astype(BF16)

    edges = [
        (t_buf.at[0], t_buf.at[1], 0, -1, 0),
        (t_buf.at[0], t_buf.at[2], 1, -1, 1),
        (t_buf.at[0], t_buf.at[3], 2, 0, 1),
        (s_buf.at[0], s_buf.at[1], 3, 0, -1),
        (s_buf.at[0], s_buf.at[2], 4, 1, -1),
        (s_buf.at[0], s_buf.at[3], 5, 1, 0),
        (t_buf.at[0, pl.ds(0, 16)], k_buf.at[0], 6, -1, -1),
        (t_buf.at[0, pl.ds(0, 16)], k_buf.at[1], 7, 0, -1),
    ]

    def inside(gg, rr):
        ok = None
        for cond in ((gg >= 0), (gg < GX), (rr >= 0), (rr < GY)):
            ok = cond if ok is None else jnp.logical_and(ok, cond)
        return ok

    for src, dst, i, dx, dy in edges:
        copy = remote(
            src, dst, edge_s.at[i], edge_r.at[i],
            (lax.rem(g + GX + dx, GX), lax.rem(r + GY + dy, GY), l),
        )

        @pl.when(inside(g + dx, r + dy))
        def _(copy=copy):
            copy.start()

    @pl.when(has_next)
    def _():
        h1(last, 8).start()
        h1(cell_planes(5), 5).start()
        h1(cell_planes(4), 4).start()

    s1_last.start()

    lane2 = iota((2 * SIDE, 2 * SIDE), 1)
    row2 = iota((2 * SIDE, 2 * SIDE), 0)
    col = lax.rem(lane2, SIDE)
    is_lerp = lane2 < SIDE
    here = jnp.where(is_lerp, 1.0 - tx, -1.0)
    there = jnp.where(is_lerp, tx, 1.0)
    top = jnp.where(row2 == col, here, jnp.where(row2 == col + 1, there, 0.0))
    rhs[...] = jnp.where(
        row2 < SIDE, top, jnp.where(col == SIDE - 1, there, 0.0)
    ).astype(BF16)

    point = lax.rem(lane, 32) - 8
    tap = lane // 32
    px_ok = jnp.logical_and(g * 16 + point >= 0, g * 16 + point < 16 * GX)
    basis_x = jnp.where(px_ok, spline(row.astype(F32) / S - point.astype(F32)), 0.0)
    for m in range(4):
        scale = jnp.full((SIDE, SIDE), float(TAPS[m, 3]), F32)
        for a in (2, 1, 0):
            scale = jnp.where(tap == a, float(TAPS[m, a]), scale)
        high, low = split(basis_x * scale)
        for half in range(2):
            rhs_x[pl.ds(m * 256 + half * 128, 128), pl.ds(0, 128)] = high
            rhs_x[pl.ds(m * 256 + half * 128, 128), pl.ds(128, 128)] = low

    q_point = iota((32, SIDE), 0) - 8
    q_ok = jnp.logical_and(r * 16 + q_point >= 0, r * 16 + q_point < 16 * GY)
    basis_y = jnp.where(
        q_ok, spline(iota((32, SIDE), 1).astype(F32) / S - q_point.astype(F32)), 0.0
    ) * (live * S ** (-1.5))
    high, low = split(basis_y)
    lhs_y[pl.ds(0, 32), pl.ds(0, 128)] = high
    lhs_y[pl.ds(0, 32), pl.ds(128, 128)] = high
    lhs_y[pl.ds(32, 32), pl.ds(0, 128)] = low
    lhs_y[pl.ds(32, 32), pl.ds(128, 128)] = jnp.zeros((32, SIDE), BF16)

    wr, wl = iota((512, SIDE), 0), iota((512, SIDE), 1)
    w_c[...] = (
        weight(wr // 32 - 4 - 2 * (wl // 16 - 1)) * weight(lax.rem(wr, 32) - 8 - 2 * (lax.rem(wl, 16) - 1))
    ).astype(BF16)

    kz = 4 * (iota((512, 16), 0) // 128) + lax.rem(iota((512, 16), 0) // 16, 8) - 1
    pick_z = (kz == iota((512, 16), 1)).astype(F32)
    spread_z = weight(l * 8 + iota((16, SIDE), 1) // 16 - 2 * iota((16, SIDE), 0))
    full_z = mm_full(mm_full(pick_z, pz[...], ((1,), (1,))), spread_z)
    full_z = jnp.where(lax.rem(wr, 16) == lax.rem(wl, 16), full_z, 0.0)
    high, low = split(full_z)
    w_z[0], w_z[1] = high, low

    jy = 8 * (iota((32, 64), 1) // 16) + lax.rem(iota((32, 64), 1), 16) - 1
    pick_y = (jy == iota((32, 64), 0)).astype(F32)
    spread_y = weight(r * 16 + iota((16, 32), 0) - 2 * iota((16, 32), 1))
    full_y = mm_full(spread_y, mm_full(py[...], pick_y))
    high, low = split(full_y)
    m_y[...] = jnp.concatenate(
        [
            jnp.concatenate([high.astype(F32), high.astype(F32)], axis=1),
            jnp.concatenate([low.astype(F32), jnp.zeros((16, 64), F32)], axis=1),
        ],
        axis=0,
    ).astype(BF16)

    xl = iota((64, 256), 1)
    x_point = lax.rem(xl, 32) - 8
    spread_x = jnp.where(
        jnp.logical_and(x_point >= 0, x_point < 16),
        weight(g * 16 + x_point - 2 * iota((64, 256), 0)),
        0.0,
    )
    prolong_x = mm_full(px[...], spread_x, ((0,), (0,)))
    same = lax.rem(iota((128, 256), 0) // 16, 8) == iota((128, 256), 1) // 32

    def x_step(dev, carry):
        kx = 8 * dev + lax.rem(iota((128, 64), 0), 16) - 1
        pick_x = (kx == iota((128, 64), 1)).astype(F32)
        full_x = jnp.where(same, mm_full(pick_x, prolong_x), 0.0)
        high, low = split(full_x)
        place = pl.ds(pl.multiple_of(dev * 128, 128), 128)
        w_x[0, place, :] = high
        w_x[1, place, :] = low
        return carry

    lax.fori_loop(0, GX, x_step, 0)

    def clear_acc(i, carry):
        acc[i] = jnp.zeros((32, 384), F32)
        return carry

    lax.fori_loop(0, 4, clear_acc, 0)

    for src, dst, i, dx, dy in edges:
        copy = remote(src, dst, edge_s.at[i], edge_r.at[i], (g, across, l))
        there_ok = inside(g - dx, r - dy)

        @pl.when(there_ok)
        def _(copy=copy):
            copy.wait_recv()

        @pl.when(jnp.logical_not(there_ok))
        def _(dst=dst):
            dst[...] = jnp.zeros(dst.shape, BF16)

    moved_x, moved_y = ox != 0, oy != 0
    both = jnp.logical_and(moved_x, moved_y)

    def pick(stay, by_x, by_y, by_both):
        return jnp.where(moved_y, jnp.where(moved_x, by_both, by_y), jnp.where(moved_x, by_x, stay))

    t_here = t_buf[0].astype(F32)
    t_right = t_buf[1].astype(F32)
    t_sel[...] = pick(t_right, t_here, t_buf[2].astype(F32), t_buf[3].astype(F32))
    s_sel = pick(
        s_buf[1].astype(F32), s_buf[2].astype(F32), s_buf[0].astype(F32), s_buf[3].astype(F32)
    )
    k_sel = pick(k_buf[0].astype(F32), k_buf[1].astype(F32), t_right[:16], t_here[:16])
    diag = jnp.where(lane[:80] == row[:80], jnp.broadcast_to(k_sel[0:1, :], (80, SIDE)), 0.0)
    bottom = mm(jnp.concatenate([s_sel, diag], axis=1).astype(BF16), rhs[...])
    a_bot[...] = bottom[:, :SIDE]
    b_bot[...] = bottom[:, SIDE:]

    s1_bulk.wait_recv()
    s1_last.wait_recv()
    flag.wait_recv()
    load_fixed.wait()

    use_own = jnp.logical_not(jnp.logical_or(moved_x, moved_y))
    only_x = jnp.logical_and(moved_x, jnp.logical_not(moved_y))
    only_y = jnp.logical_and(moved_y, jnp.logical_not(moved_x))
    use_land = jnp.logical_or(
        only_x,
        jnp.logical_or(jnp.logical_and(r == 2, only_y), jnp.logical_and(r == 3, both)),
    )
    use_sib1 = jnp.logical_and(lax.rem(r, 2) == 1, only_y)
    use_sib2 = jnp.logical_and(r == 2, both)
    use_sib3 = jnp.logical_and(r == 1, both)

    def choose(z):
        value = jnp.where(use_sib3, sib3[z], jnp.zeros((SIDE, SIDE), BF16))
        value = jnp.where(use_sib2, sib2[z], value)
        value = jnp.where(use_sib1, sib1[z], value)
        value = jnp.where(use_land, land[z], value)
        return jnp.where(use_own, own[z], value)

    def forward(sl, i, start, count):
        @pl.when(has_prev)
        def _():
            h1(sl, i).wait_recv()

        @pl.when(jnp.logical_or(r == 0, r == 3))
        def _():
            s2(sl, i).start()

        @pl.when(r == 1)
        def _():
            s2(sl, i).wait_recv()

        def blend(other):
            def step(j, carry):
                z = start + j
                m = flag_in[...]
                stage[z] = other[z] * m + relay[z] * (1.0 - m).astype(BF16)
                return carry

            lax.fori_loop(0, count, step, 0)

        @pl.when(r == 0)
        def _():
            blend(sib1)
            h2(stage, sl, i).start()

        @pl.when(r == 1)
        def _():
            blend(sib2)
            h2(stage, sl, i).start()

        @pl.when(r >= 2)
        def _():
            h2(relay, sl, i).start()

    def landing(sl, i):
        h2(relay, sl, i).wait_recv()

        @pl.when(r == 0)
        def _():
            s3(sl, i).start()

        @pl.when(r == 1)
        def _():
            s3(sl, i).wait_recv()

        @pl.when(r == 2)
        def _():
            s2(sl, i).wait_recv()

    def fill(z, j):
        lhs[pl.ds(j * SIDE, SIDE), pl.ds(0, SIDE)] = choose(z)
        lhs[pl.ds(j * SIDE, SIDE), pl.ds(SIDE, SIDE)] = jnp.where(lane == z, t_sel[...], 0.0).astype(BF16)

    def lerp_x(z, j, slot):
        both_x = mm(lhs[pl.ds(j * SIDE, SIDE), :], rhs[...])
        a_buf[slot, pl.ds(0, SIDE), :] = both_x[:, :SIDE]
        b_buf[slot, pl.ds(0, SIDE), :] = both_x[:, SIDE:]
        a_buf[slot, pl.ds(SIDE, 1), :] = a_bot[pl.ds(z, 1), :]
        b_buf[slot, pl.ds(SIDE, 1), :] = b_bot[pl.ds(z, 1), :]

    def rows_of(j, y0):
        a = a_buf[j, pl.ds(y0, 16), :]
        b = b_buf[j, pl.ds(y0, 16), :]
        dy = a_buf[j, pl.ds(y0 + 1, 16), :] - a
        along_xy = a + ty * dy
        diff_xy = b + ty * (b_buf[j, pl.ds(y0 + 1, 16), :] - b)
        return along_xy, diff_xy, dy

    def compute(k):
        for j in range(S):
            fill(k * S + j, j)
        for j in range(S):
            lerp_x(k * S + j, j, j)

        def tile(t, carry):
            y0 = pl.multiple_of(t * 16, 16)
            w1, x1, y1 = rows_of(S, y0)
            sums = [[jnp.zeros((16, SIDE), F32) for _ in range(4)] for _ in range(3)]
            for j in reversed(range(S)):
                w0, x0, yy0 = rows_of(j, y0)
                gz = w1 - w0
                res = w0 + tz * gz - fixed[k * S + j, pl.ds(y0, 16), :].astype(F32)
                grads = (x0 + tz * (x1 - x0), yy0 + tz * (y1 - yy0), gz)
                for d in range(3):
                    value = res * grads[d]
                    for m in range(4):
                        value = sums[d][m] + value
                        sums[d][m] = value
                w1, x1, y1 = w0, x0, yy0
            for d in range(3):
                for m in range(4):
                    high, low = split(sums[d][m])
                    place = pl.ds(pl.multiple_of(d * SIDE + y0, 16), 16)
                    mom[place, pl.ds(m * 256, 128)] = high
                    mom[place, pl.ds(m * 256 + 128, 128)] = low
            return carry

        lax.fori_loop(0, SIDE // 16, tile, 0)
        a_buf[S] = a_buf[0]
        b_buf[S] = b_buf[0]

        parts = mm(mom[...], rhs_x[...])
        parts = parts[:, :SIDE] + parts[:, SIDE:]
        wide = jnp.concatenate([parts[d * SIDE:(d + 1) * SIDE] for d in range(3)], axis=1)
        high, low = split(wide)
        h_x[pl.ds(0, SIDE), :] = high
        h_x[pl.ds(SIDE, SIDE), :] = low
        done = mm(lhs_y[...], h_x[...])
        done = done[:32] + done[32:]
        turn = lax.rem(k + 3, 4)
        base = (k + 3) // 4
        blocks = iota((32, SIDE), 1) // 32
        for d in range(3):
            moved = pltpu.roll(done[:, d * SIDE:(d + 1) * SIDE], turn * 32, 1)
            place = pl.ds(d * SIDE, SIDE)
            acc[base, :, place] += jnp.where(blocks >= turn, moved, 0.0)
            acc[base + 1, :, place] += jnp.where(blocks < turn, moved, 0.0)

    forward(cell_planes(7), 7, 56, S)
    forward(last, 8, DEPTH, 1)
    landing(last, 8)
    fill(DEPTH, 0)
    lerp_x(DEPTH, 0, S)

    def step(n, carry):
        k = 7 - n

        @pl.when(jnp.logical_and(k >= 4, has_next))
        def _():
            h1(cell_planes(k - 4), k - 4).start()

        @pl.when(k >= 1)
        def _():
            forward(cell_planes(k - 1), k - 1, (k - 1) * S, S)

        landing(cell_planes(k), k)
        compute(k)
        return carry

    lax.fori_loop(0, CELLS, step, 0)

    up_z = remote(acc.at[3], f_z.at[0], fine_s.at[0], fine_r.at[0], (g, r, lax.rem(l + 1, GZ)))
    down_z = remote(acc.at[0], f_z.at[1], fine_s.at[1], fine_r.at[1], (g, r, lax.rem(l + GZ - 1, GZ)))

    @pl.when(above)
    def _():
        up_z.start()

    @pl.when(below)
    def _():
        down_z.start()

    keep = [below.astype(F32), 1.0, 1.0, above.astype(F32)]
    groups = [acc[i] * keep[i] if i in (0, 3) else acc[i] for i in range(4)]
    stacked = jnp.concatenate(
        [jnp.concatenate([grp[:, d * SIDE:(d + 1) * SIDE] for grp in groups], axis=1) for d in range(3)],
        axis=0,
    )
    high, low = split(stacked)
    restricted = mm(high, w_c[...]) + mm(low, w_c[...])
    wide = jnp.concatenate([restricted[d * 32:(d + 1) * 32] for d in range(3)], axis=1)
    high, low = split(wide)
    r_y = weight(iota((16, 32), 1) - 8 - 2 * (iota((16, 32), 0) - 1)).astype(BF16)
    c_z[l] = mm(r_y, high) + mm(r_y, low)

    def spread(buf, sems, axis, size, index):
        copies = []
        for o in range(1, size):
            where = {"gx": (lax.rem(g + o, size), r, l), "gy": (g, lax.rem(r + o, size), l), "gz": (g, r, lax.rem(l + o, size))}[axis]
            copies.append(remote(buf.at[index], buf.at[index], sems[0].at[o], sems[1].at[index], where))
        return copies

    def arrivals(buf, sems, size, index):
        for o in range(1, size):
            other = lax.rem(index + o, size)
            remote(buf.at[other], buf.at[other], sems[0].at[o], sems[1].at[other], partner).wait_recv()

    z_copies = spread(c_z, (cz_s, cz_r), "gz", GZ, l)
    for copy in z_copies:
        copy.start()

    fold[...] = acc[pl.ds(1, 2)]

    @pl.when(below)
    def _():
        up_z.wait_recv()
        fold[0] += f_z[0]

    @pl.when(above)
    def _():
        down_z.wait_recv()
        fold[1] += f_z[1]

    up_y = remote(fold.at[:, pl.ds(24, 8)], f_y.at[0], fine_s.at[2], fine_r.at[2], (g, lax.rem(r + 1, GY), l))
    down_y = remote(fold.at[:, pl.ds(0, 8)], f_y.at[1], fine_s.at[3], fine_r.at[3], (g, lax.rem(r + GY - 1, GY), l))
    has_low, has_high = r > 0, r < GY - 1

    @pl.when(has_high)
    def _():
        up_y.start()

    @pl.when(has_low)
    def _():
        down_y.start()

    arrivals(c_z, (cz_s, cz_r), GZ, l)
    gathered = jnp.concatenate(
        [
            jnp.concatenate([c_z[dev, :, pl.ds(d * SIDE, SIDE)] for dev in range(GZ)], axis=1)
            for d in range(3)
        ],
        axis=0,
    )
    high, low = split(gathered)
    c_y[r] = mm(high, w_z[0]) + mm(low, w_z[0]) + mm(high, w_z[1])
    y_copies = spread(c_y, (cy_s, cy_r), "gy", GY, r)
    for copy in y_copies:
        copy.start()

    @pl.when(has_low)
    def _():
        up_y.wait_recv()
        fold[:, pl.ds(8, 8), :] += f_y[0]

    @pl.when(has_high)
    def _():
        down_y.wait_recv()
        fold[:, pl.ds(16, 8), :] += f_y[1]

    middle = pl.ds(8, 16)
    up_x = remote(fold.at[:, middle], f_x.at[0], fine_s.at[4], fine_r.at[4], (lax.rem(g + 1, GX), r, l))
    down_x = remote(fold.at[:, middle], f_x.at[1], fine_s.at[5], fine_r.at[5], (lax.rem(g + GX - 1, GX), r, l))

    @pl.when(has_next)
    def _():
        up_x.start()

    @pl.when(has_prev)
    def _():
        down_x.start()

    arrivals(c_y, (cy_s, cy_r), GY, r)
    gathered = jnp.concatenate(
        [
            jnp.concatenate([c_y[dev, pl.ds(d * 16, 16), :] for d in range(3)], axis=1)
            for dev in range(GY)
        ],
        axis=0,
    )
    high, low = split(gathered)
    both_y = mm(m_y[...], jnp.concatenate([high, low], axis=0))
    c_x[g] = both_y[:16] + both_y[16:]
    x_copies = spread(c_x, (cx_s, cx_r), "gx", GX, g)
    for copy in x_copies:
        copy.start()

    @pl.when(jnp.logical_not(has_prev))
    def _():
        f_x[0] = jnp.zeros(f_x.shape[1:], F32)

    @pl.when(jnp.logical_not(has_next))
    def _():
        f_x[1] = jnp.zeros(f_x.shape[1:], F32)

    @pl.when(has_prev)
    def _():
        up_x.wait_recv()

    @pl.when(has_next)
    def _():
        down_x.wait_recv()

    spot = lax.rem(iota((16, SIDE), 1), 32)
    fine = []
    for half in range(2):
        for d in range(3):
            cols = pl.ds(d * SIDE, SIDE)
            value = fold[half, middle, cols]
            left = pltpu.roll(f_x[0, half, :, cols], SIDE - 16, 1)
            right = pltpu.roll(f_x[1, half, :, cols], 16, 1)
            value = value + jnp.where(jnp.logical_or(spot == 8, spot == 9), left, 0.0)
            fine.append(value + jnp.where(spot == 23, right, 0.0))

    arrivals(c_x, (cx_s, cx_r), GX, g)
    gathered = jnp.concatenate(
        [
            jnp.concatenate([c_x[dev, :, pl.ds(d * SIDE, SIDE)] for dev in range(GX)], axis=1)
            for d in range(3)
        ],
        axis=0,
    )
    high, low = split(gathered)
    corr = mm(high, w_x[0]) + mm(low, w_x[0]) + mm(high, w_x[1])
    for half in range(2):
        for d in range(3):
            total = fine[half * 3 + d] + corr[d * 16:(d + 1) * 16, half * SIDE:(half + 1) * SIDE]
            for b in range(4):
                out[d, half * 4 + b] = total[:, b * 32 + 8:b * 32 + 24]

    @pl.when(below)
    def _():
        plane.wait_send()
        down_z.wait_send()

    @pl.when(above)
    def _():
        up_z.wait_send()

    @pl.when(has_low)
    def _():
        down_y.wait_send()

    @pl.when(has_high)
    def _():
        up_y.wait_send()

    @pl.when(has_prev)
    def _():
        down_x.wait_send()

    @pl.when(has_next)
    def _():
        up_x.wait_send()
        h1(last, 8).wait_send()

    flag.wait_send()
    s1_bulk.wait_send()
    s1_last.wait_send()
    for src, dst, i, dx, dy in edges:
        copy = remote(src, dst, edge_s.at[i], edge_r.at[i], partner)

        @pl.when(inside(g + dx, r + dy))
        def _(copy=copy):
            copy.wait_send()

    for copy in z_copies + y_copies + x_copies:
        copy.wait_send()

    def drain(sl, i):
        h2(relay, sl, i).wait_send()

        @pl.when(jnp.logical_or(r == 0, r == 3))
        def _():
            s2(sl, i).wait_send()

        @pl.when(r == 0)
        def _():
            s3(sl, i).wait_send()

    drain(last, 8)

    def drain_cell(k, carry):
        @pl.when(has_next)
        def _():
            h1(cell_planes(k), k).wait_send()

        drain(cell_planes(k), k)
        return carry

    lax.fori_loop(0, CELLS, drain_cell, 0)


def per_device(
    fixed_image, moving_image, block_shift, fraction, brick_valid, precond_x, precond_y, precond_z
):
    dma = pltpu.SemaphoreType.DMA
    vmem = pltpu.VMEM
    brick = vmem((DEPTH + 1, SIDE, SIDE), BF16)
    any_spec = pl.BlockSpec(memory_space=pl.ANY)
    smem_spec = pl.BlockSpec(memory_space=pltpu.SMEM)
    vmem_spec = pl.BlockSpec(memory_space=pltpu.VMEM)
    return pl.pallas_call(
        kernel,
        out_shape=jax.ShapeDtypeStruct((3, 8, 16, 16), F32),
        in_specs=[any_spec, any_spec, smem_spec, smem_spec, smem_spec, vmem_spec, vmem_spec, vmem_spec],
        out_specs=vmem_spec,
        scratch_shapes=[
            brick, brick, brick, brick, brick, brick, brick,
            vmem((DEPTH, SIDE, SIDE), BF16),
            vmem((SIDE, SIDE), BF16), vmem((SIDE, SIDE), BF16),
            vmem((4, SIDE, SIDE), BF16), vmem((4, 80, SIDE), BF16), vmem((2, 16, SIDE), BF16),
            vmem((SIDE, SIDE), F32), vmem((80, SIDE), F32), vmem((80, SIDE), F32),
            vmem((S * SIDE, 256), BF16), vmem((256, 256), BF16),
            vmem((S + 1, SIDE + 8, SIDE), F32), vmem((S + 1, SIDE + 8, SIDE), F32),
            vmem((3 * SIDE, 1024), BF16), vmem((1024, 256), BF16), vmem((64, 256), BF16),
            vmem((4, 32, 384), F32), vmem((512, SIDE), BF16),
            vmem((2, 512, SIDE), BF16), vmem((2, 1024, 256), BF16), vmem((32, SIDE), BF16),
            vmem((GZ, 16, 384), F32), vmem((GY, 48, SIDE), F32), vmem((GX, 16, 384), F32),
            vmem((2, 32, 384), F32), vmem((2, 2, 8, 384), F32), vmem((2, 2, 16, 384), F32),
            vmem((2, 32, 384), F32), vmem((256, 384), BF16),
            dma((2,)),
            dma((9,)), dma((9,)), dma((9,)), dma((9,)),
            dma((2,)), dma((2,)), dma((9,)), dma((9,)), dma((9,)), dma((9,)),
            dma((10,)), dma((10,)), dma((6,)), dma((6,)),
            dma((GZ,)), dma((GZ,)), dma((GY,)), dma((GY,)), dma((GX,)), dma((GX,)),
        ],
        compiler_params=pltpu.CompilerParams(
            collective_id=0, has_side_effects=True, vmem_limit_bytes=48 * 2**20
        ),
        name="registration_gradient",
    )(moving_image, fixed_image, block_shift, fraction, brick_valid, precond_x, precond_y, precond_z)


def solution(mesh):
    return jax.shard_map(
        per_device,
        mesh=mesh,
        in_specs=(
            P("gz", "gy", "gx"),
            P("gz", "gy", "gx"),
            P(None, "gz", "gy", "gx"),
            P(None, "gz", "gy", "gx"),
            P("gz", "gy", "gx"),
            P(),
            P(),
            P(),
        ),
        out_specs=P(None, "gz", "gy", "gx"),
        check_vma=False,
    )
```

```python
import jax
import jax.numpy as jnp
import numpy as np
from jax import lax
from jax.experimental import pallas as pl
from jax.experimental.pallas import tpu as pltpu
from jax.sharding import PartitionSpec as P

S = 8
SIDE = 128
DEPTH = 64
CELLS = DEPTH // S
HALF = S // 2
AHEAD = 3
PIECES = 2 * CELLS + 1
GX, GY, GZ = 8, 4, 4
FULL = lax.Precision.HIGHEST
F32 = jnp.float32
BF16 = jnp.bfloat16
MESH = pl.DeviceIdType.MESH


def tap_polynomials():
    j = np.arange(S, dtype=np.float64)
    basis = np.stack(
        [np.ones(S), j + 1, (j + 1) * (j + 2) / 2, (j + 1) * (j + 2) * (j + 3) / 6], axis=1
    )
    taps = []
    for a in range(4):
        u = np.abs(j / S - (a - 1))
        taps.append(
            np.where(u < 1, 2 / 3 - u**2 + u**3 / 2, np.where(u < 2, (2 - u) ** 3 / 6, 0.0))
        )
    return np.linalg.lstsq(basis, np.stack(taps, axis=1), rcond=None)[0]


TAPS = tap_polynomials()


def iota(shape, dim):
    return lax.broadcasted_iota(jnp.int32, shape, dim)


def spline(distance):
    dist = jnp.abs(distance)
    inner = 2.0 / 3.0 - dist * dist + dist * dist * dist / 2.0
    far = 2.0 - dist
    outer = far * far * far / 6.0
    return jnp.where(dist < 1.0, inner, jnp.where(dist < 2.0, outer, 0.0))


def weight(gap):
    gap = jnp.abs(gap)
    return jnp.where(gap == 0, 0.75, jnp.where(gap == 1, 0.5, jnp.where(gap == 2, 0.125, 0.0)))


def split(value):
    high = value.astype(BF16)
    return high, (value - high.astype(F32)).astype(BF16)


def mm(a, b):
    return jnp.dot(a, b, preferred_element_type=F32)


def mm_full(a, b, dims=((1,), (0,))):
    return lax.dot_general(a, b, (dims, ((), ())), precision=FULL, preferred_element_type=F32)


def kernel(
    mov, fix, shift_h, frac_h, valid_h, px_h, py_h, pz_h, out,
    shift, frac, valid, px, py, pz,
    own, relay, land, stage, sib1, sib2, fixed,
    flag_out, flag_in, e_own, e_x, e_up, e_up_x, e_down, e_down_x, t_sel, a_bot, b_bot,
    lhs, rhs, a_buf, b_buf, mom, rhs_x, lhs_y, acc, coarse, w_c,
    w_z, w_x, m_y, c_z, c_y, c_x, top_out, top_in, low_out, low_in, f_y, x_out, x_in, fold, h_x,
    local_sem, h1_s, h1_r, h2_s, h2_r, s1_s, s1_r, s2_s, s2_r,
    edge_s, edge_r, fine_s, fine_r, cz_s, cz_r, cy_s, cy_r, cx_s, cx_r,
):
    g, r, l = lax.axis_index("gx"), lax.axis_index("gy"), lax.axis_index("gz")
    across = lax.rem(r + 2, GY)
    sibling = (g, r + 1 - 2 * lax.rem(r, 2), l)
    partner = (g, across, l)

    def remote(src, dst, send, recv, device):
        return pltpu.make_async_remote_copy(
            src_ref=src, dst_ref=dst, send_sem=send, recv_sem=recv,
            device_id=device, device_id_type=MESH,
        )

    smalls = [
        pltpu.make_async_copy(src, dst, local_sem.at[2 + i])
        for i, (src, dst) in enumerate(
            ((shift_h, shift), (frac_h, frac), (valid_h, valid), (px_h, px), (py_h, py), (pz_h, pz))
        )
    ]
    for copy in smalls:
        copy.start()
    load_own = pltpu.make_async_copy(mov, own.at[pl.ds(0, DEPTH)], local_sem.at[0])
    load_fixed = pltpu.make_async_copy(fix, fixed, local_sem.at[1])
    load_own.start()
    load_fixed.start()

    peers = [(lax.rem(g + o, GX), r, l) for o in range(1, GX)]
    peers += [(g, lax.rem(r + o, GY), l) for o in range(1, GY)]
    peers += [(g, r, lax.rem(l + o, GZ)) for o in range(1, GZ)]
    peers += [(lax.rem(g + o, GX), across, l) for o in (1, GX - 1)]
    barrier = pltpu.get_barrier_semaphore()
    for peer in peers:
        pl.semaphore_signal(barrier, inc=1, device_id=peer, device_id_type=MESH)
    for copy in smalls:
        copy.wait()
    ox, oy = shift[0], shift[1]
    tx = frac[0].astype(F32) / 64.0
    ty = frac[1].astype(F32) / 64.0
    tz = frac[2].astype(F32) / 64.0
    live = valid[0, 0, 0].astype(F32)
    flag_out[...] = jnp.full((SIDE, SIDE), -oy.astype(F32), F32).astype(BF16)
    pl.semaphore_wait(barrier, len(peers))

    def part(k, h):
        return pl.ds(pl.multiple_of(k * S + h * HALF, HALF), HALF), 2 * k + h

    last = (pl.ds(DEPTH, 1), 2 * CELLS)

    def h1(piece, src=None):
        sl, i = piece
        if src is None:
            src = own if piece is last else mov
        return remote(
            src.at[sl], relay.at[sl], h1_s.at[i], h1_r.at[i], (lax.rem(g + 1, GX), across, l)
        )

    def h2(src, piece):
        sl, i = piece
        return remote(src.at[sl], land.at[sl], h2_s.at[i], h2_r.at[i], partner)

    def s1(piece):
        sl, i = piece
        src = own if piece is last else mov
        return remote(src.at[sl], sib1.at[sl], s1_s.at[i], s1_r.at[i], sibling)

    def s2(src, piece):
        sl, i = piece
        return remote(src.at[sl], sib2.at[sl], s2_s.at[i], s2_r.at[i], sibling)

    has_next, has_prev = g < GX - 1, g > 0
    above, below = l < GZ - 1, l > 0
    has_low, has_high = r > 0, r < GY - 1
    row0, row1, row2, row3 = (r == i for i in range(4))
    either = jnp.logical_or

    left = (lax.rem(g + GX - 1, GX), r, l)
    right = (lax.rem(g + 1, GX), r, l)
    low_row = (g, lax.rem(r + GY - 1, GY), l)
    high_row = (g, lax.rem(r + 1, GY), l)
    low_slab = (g, r, lax.rem(l + GZ - 1, GZ))
    high_slab = (g, r, lax.rem(l + 1, GZ))

    plane = remote(mov.at[pl.ds(0, 1)], own.at[last[0]], edge_s.at[6], edge_r.at[6], low_slab)
    flag_up = remote(flag_out, flag_in, edge_s.at[7], edge_r.at[7], partner)
    flag_left = remote(flag_out, flag_in, edge_s.at[7], edge_r.at[7], left)
    asks_left = jnp.logical_and(row3, has_prev)
    asked = jnp.logical_and(row3, has_next)

    @pl.when(below)
    def _():
        plane.start()

    @pl.when(row2)
    def _():
        flag_up.start()

    @pl.when(asks_left)
    def _():
        flag_left.start()

    @pl.when(jnp.logical_not(row3))
    def _():
        for h in (1, 0):
            s1(part(7, h)).start()

    def blend(first, second, sl, count):
        def step(j, carry):
            z = sl.start + j
            m = flag_in[...]
            stage[z] = first[z] * m + second[z] * (1.0 - m).astype(BF16)
            return carry

        lax.fori_loop(0, count, step, 0)

    def send(piece, count):
        @pl.when(jnp.logical_and(has_next, jnp.logical_not(row3)))
        def _():
            h1(piece).start()

        @pl.when(row3)
        def _():
            s1(piece).wait_recv()

        @pl.when(asked)
        def _():
            blend(sib1, own, piece[0], count)
            h1(piece, stage).start()

    @pl.when(jnp.logical_and(has_next, jnp.logical_not(row3)))
    def _():
        for n in range(AHEAD):
            h1(part(7 - n // 2, 1 - n % 2)).start()

    zero_plane = jnp.zeros((1, SIDE, SIDE), BF16)

    @pl.when(jnp.logical_not(above))
    def _():
        own[pl.ds(DEPTH, 1)] = zero_plane

    @pl.when(jnp.logical_not(has_prev))
    def _():
        def clear(z, carry):
            relay[pl.ds(z, 1)] = zero_plane
            return carry

        lax.fori_loop(0, DEPTH + 1, clear, 0)

    load_own.wait()

    @pl.when(asked)
    def _():
        flag_left.wait_recv()

    @pl.when(row3)
    def _():
        for n in range(AHEAD - 1):
            send(part(7 - n // 2, 1 - n % 2), HALF)

    lane = iota((SIDE, SIDE), 1)
    row = iota((SIDE, SIDE), 0)

    def edge_step(z, carry):
        t, s = carry
        value = own[z].astype(F32)
        t = jnp.where(lane == z, jnp.broadcast_to(value[:, 0:1], (SIDE, SIDE)), t)
        s = jnp.where(row[:80] == z, jnp.broadcast_to(value[0:1, :], (80, SIDE)), s)
        return t, s

    t_own, s_own = lax.fori_loop(
        0, DEPTH, edge_step, (jnp.zeros((SIDE, SIDE), F32), jnp.zeros((80, SIDE), F32))
    )

    @pl.when(above)
    def _():
        plane.wait_recv()

    t_own, s_own = edge_step(DEPTH, (t_own, s_own))
    rows_s, rows_t = pl.ds(0, 80), pl.ds(80, 80)
    e_own[rows_s, :] = s_own.astype(BF16)
    e_own[rows_t, :] = jnp.transpose(t_own)[:80].astype(BF16)

    s_right = remote(e_own.at[rows_s], e_x.at[rows_s], edge_s.at[0], edge_r.at[0], right)
    t_left = remote(e_own.at[rows_t], e_x.at[rows_t], edge_s.at[1], edge_r.at[1], left)
    own_low = remote(e_own, e_up, edge_s.at[2], edge_r.at[2], low_row)
    x_low = remote(e_x, e_up_x, edge_s.at[3], edge_r.at[3], low_row)
    own_high = remote(e_own.at[rows_t], e_down, edge_s.at[4], edge_r.at[4], high_row)
    x_high = remote(e_x.at[rows_t], e_down_x, edge_s.at[5], edge_r.at[5], high_row)

    @pl.when(has_next)
    def _():
        s_right.start()

    @pl.when(has_prev)
    def _():
        t_left.start()

    @pl.when(has_low)
    def _():
        own_low.start()

    @pl.when(has_high)
    def _():
        own_high.start()

    @pl.when(jnp.logical_not(row3))
    def _():
        s1(last).start()
        for k in (6, 5):
            for h in (1, 0):
                s1(part(k, h)).start()

    send(last, 1)

    moved_x, moved_y = ox != 0, oy != 0
    both = jnp.logical_and(moved_x, moved_y)

    use_own = jnp.logical_not(jnp.logical_or(moved_x, moved_y))
    only_x = jnp.logical_and(moved_x, jnp.logical_not(moved_y))
    only_y = jnp.logical_and(moved_y, jnp.logical_not(moved_x))
    use_land = either(
        only_x, either(jnp.logical_and(row2, only_y), jnp.logical_and(row3, both))
    )
    use_sib1 = jnp.logical_and(either(row1, row3), only_y)
    use_sib2 = jnp.logical_and(either(row1, row2), both)

    def choose(z):
        value = jnp.where(use_sib2, sib2[z], jnp.zeros((SIDE, SIDE), BF16))
        value = jnp.where(use_sib1, sib1[z], value)
        value = jnp.where(use_land, land[z], value)
        return jnp.where(use_own, own[z], value)

    def forward(piece, count, k=None, h=None):
        @pl.when(has_prev)
        def _():
            h1(piece).wait_recv()

        @pl.when(row0)
        def _():
            s1(piece).wait_recv()
            blend(sib1, relay, piece[0], count)
            h2(stage, piece).start()

        @pl.when(jnp.logical_not(row0))
        def _():
            h2(relay, piece).start()

        @pl.when(row3)
        def _():
            s2(relay, piece).start()

        if k is not None:
            later = 2 * (7 - k) + (1 - h) + AHEAD

            @pl.when(later < 2 * CELLS)
            def _():
                send(part(7 - later // 2, 1 - lax.rem(later, 2)), HALF)

    def landing(piece):
        h2(relay, piece).wait_recv()

        @pl.when(row0)
        def _():
            s2(land, piece).start()

        @pl.when(row1)
        def _():
            s1(piece).wait_recv()

        @pl.when(either(row1, row2))
        def _():
            s2(relay, piece).wait_recv()

    up_z = remote(top_out, top_in, fine_s.at[0], fine_r.at[0], high_slab)

    @pl.when(row0)
    def _():
        flag_up.wait_recv()

    @pl.when(row3)
    def _():
        send(part(7 - (AHEAD - 1) // 2, 1 - (AHEAD - 1) % 2), HALF)

    forward(part(7, 1), HALF, 7, 1)

    rhs_lane = iota((2 * SIDE, 2 * SIDE), 1)
    rhs_row = iota((2 * SIDE, 2 * SIDE), 0)
    col = lax.rem(rhs_lane, SIDE)
    is_lerp = rhs_lane < SIDE
    here = jnp.where(is_lerp, 1.0 - tx, -1.0)
    there = jnp.where(is_lerp, tx, 1.0)
    top = jnp.where(rhs_row == col, here, jnp.where(rhs_row == col + 1, there, 0.0))
    rhs[...] = jnp.where(
        rhs_row < SIDE, top, jnp.where(col == SIDE - 1, there, 0.0)
    ).astype(BF16)

    point = lax.rem(lane, 32) - 8
    tap = lane // 32
    px_ok = jnp.logical_and(g * 16 + point >= 0, g * 16 + point < 16 * GX)
    basis_x = jnp.where(px_ok, spline(row.astype(F32) / S - point.astype(F32)), 0.0)
    for m in range(4):
        scale = jnp.full((SIDE, SIDE), float(TAPS[m, 3]), F32)
        for a in (2, 1, 0):
            scale = jnp.where(tap == a, float(TAPS[m, a]), scale)
        high, low = split(basis_x * scale)
        for half in range(2):
            rhs_x[pl.ds(m * 256 + half * 128, 128), pl.ds(0, 128)] = high
            rhs_x[pl.ds(m * 256 + half * 128, 128), pl.ds(128, 128)] = low

    q_point = iota((32, SIDE), 0) - 8
    q_ok = jnp.logical_and(r * 16 + q_point >= 0, r * 16 + q_point < 16 * GY)
    basis_y = jnp.where(
        q_ok, spline(iota((32, SIDE), 1).astype(F32) / S - q_point.astype(F32)), 0.0
    ) * (live * S ** (-1.5))
    high, low = split(basis_y)
    lhs_y[pl.ds(0, 32), pl.ds(0, 128)] = high
    lhs_y[pl.ds(0, 32), pl.ds(128, 128)] = high
    lhs_y[pl.ds(32, 32), pl.ds(0, 128)] = low
    lhs_y[pl.ds(32, 32), pl.ds(128, 128)] = jnp.zeros((32, SIDE), BF16)

    coarse_y = mm_full(weight(iota((16, 32), 1) - 8 - 2 * (iota((16, 32), 0) - 1)), basis_y)
    high, low = split(coarse_y)
    lhs_y[pl.ds(64, 16), pl.ds(0, 128)] = high
    lhs_y[pl.ds(64, 16), pl.ds(128, 128)] = high
    lhs_y[pl.ds(80, 16), pl.ds(0, 128)] = low
    lhs_y[pl.ds(80, 16), pl.ds(128, 128)] = jnp.zeros((16, SIDE), BF16)

    def cell_weights(k, carry):
        z_point = k + row // 32 - 1
        z_ok = jnp.logical_and(l * 8 + z_point >= 0, l * 8 + z_point < 8 * GZ)
        both_w = weight(z_point - 2 * (lane // 16 - 1)) * weight(
            lax.rem(row, 32) - 8 - 2 * (lax.rem(lane, 16) - 1)
        )
        w_c[k] = jnp.where(z_ok, both_w, 0.0).astype(BF16)
        return carry

    lax.fori_loop(0, CELLS, cell_weights, 0)
    coarse[...] = jnp.zeros((48, SIDE), F32)
    wr, wl = iota((512, SIDE), 0), iota((512, SIDE), 1)

    forward(part(7, 0), HALF, 7, 0)

    def arrive(copy, dst, ok):
        @pl.when(ok)
        def _():
            copy.wait_recv()

        @pl.when(jnp.logical_not(ok))
        def _():
            dst[...] = jnp.zeros(dst.shape, BF16)

    arrive(s_right, e_x.at[rows_s], has_prev)
    arrive(t_left, e_x.at[rows_t], has_next)

    @pl.when(has_low)
    def _():
        x_low.start()

    @pl.when(has_high)
    def _():
        x_high.start()

    kz = 4 * (iota((512, 16), 0) // 128) + lax.rem(iota((512, 16), 0) // 16, 8) - 1
    pick_z = (kz == iota((512, 16), 1)).astype(F32)
    spread_z = weight(l * 8 + iota((16, SIDE), 1) // 16 - 2 * iota((16, SIDE), 0))
    full_z = mm_full(mm_full(pick_z, pz[...], ((1,), (1,))), spread_z)
    full_z = jnp.where(lax.rem(wr, 16) == lax.rem(wl, 16), full_z, 0.0)
    high, low = split(full_z)
    w_z[0], w_z[1] = high, low

    jy = 8 * (iota((32, 64), 1) // 16) + lax.rem(iota((32, 64), 1), 16) - 1
    pick_y = (jy == iota((32, 64), 0)).astype(F32)
    spread_y = weight(r * 16 + iota((16, 32), 0) - 2 * iota((16, 32), 1))
    full_y = mm_full(spread_y, mm_full(py[...], pick_y))
    high, low = split(full_y)
    m_y[...] = jnp.concatenate(
        [
            jnp.concatenate([high.astype(F32), high.astype(F32)], axis=1),
            jnp.concatenate([low.astype(F32), jnp.zeros((16, 64), F32)], axis=1),
        ],
        axis=0,
    ).astype(BF16)

    xl = iota((64, 256), 1)
    x_point = lax.rem(xl, 32) - 8
    spread_x = jnp.where(
        jnp.logical_and(x_point >= 0, x_point < 16),
        weight(g * 16 + x_point - 2 * iota((64, 256), 0)),
        0.0,
    )
    prolong_x = mm_full(px[...], spread_x, ((0,), (0,)))
    same = lax.rem(iota((128, 256), 0) // 16, 8) == iota((128, 256), 1) // 32

    def x_step(dev, carry):
        kx = 8 * dev + lax.rem(iota((128, 64), 0), 16) - 1
        pick_x = (kx == iota((128, 64), 1)).astype(F32)
        full_x = jnp.where(same, mm_full(pick_x, prolong_x), 0.0)
        high, low = split(full_x)
        place = pl.ds(pl.multiple_of(dev * 128, 128), 128)
        w_x[0, place, :] = high
        w_x[1, place, :] = low
        return carry

    lax.fori_loop(0, GX, x_step, 0)

    def clear_acc(i, carry):
        acc[i] = jnp.zeros((32, 384), F32)
        return carry

    lax.fori_loop(0, 4, clear_acc, 0)

    arrive(own_low, e_up, has_high)
    arrive(own_high, e_down, has_low)
    arrive(x_low, e_up_x, has_high)
    arrive(x_high, e_down_x, has_low)

    def pick(stay, by_x, by_y, by_both):
        return jnp.where(moved_y, jnp.where(moved_x, by_both, by_y), jnp.where(moved_x, by_x, stay))

    def wide(ref, rows):
        return ref[rows, :].astype(F32)

    t_here, t_right = wide(e_own, rows_t), wide(e_x, rows_t)
    t_wide = pick(t_right, t_here, e_down_x[...].astype(F32), e_down[...].astype(F32))
    t_sel[...] = jnp.transpose(jnp.concatenate([t_wide, jnp.zeros((48, SIDE), F32)], axis=0))
    s_sel = pick(wide(e_up, rows_s), wide(e_up_x, rows_s), wide(e_own, rows_s), wide(e_x, rows_s))
    k_sel = pick(wide(e_up_x, rows_t), wide(e_up, rows_t), t_right, t_here)
    diag = jnp.where(lane[:80] == row[:80], jnp.broadcast_to(k_sel[:, 0:1], (80, SIDE)), 0.0)
    bottom = mm(jnp.concatenate([s_sel, diag], axis=1).astype(BF16), rhs[...])
    a_bot[...] = bottom[:, :SIDE]
    b_bot[...] = bottom[:, SIDE:]

    load_fixed.wait()

    def fill(z, j):
        lhs[pl.ds(j * SIDE, SIDE), pl.ds(0, SIDE)] = choose(z)
        lhs[pl.ds(j * SIDE, SIDE), pl.ds(SIDE, SIDE)] = jnp.where(lane == z, t_sel[...], 0.0).astype(BF16)

    def lerp_x(z, slot, count):
        for j in range(count):
            fill(z + j, j)
        both_x = mm(lhs[pl.ds(0, count * SIDE), :], rhs[...])
        for j in range(count):
            rows = slice(j * SIDE, (j + 1) * SIDE)
            a_buf[slot + j, pl.ds(0, SIDE), :] = both_x[rows, :SIDE]
            b_buf[slot + j, pl.ds(0, SIDE), :] = both_x[rows, SIDE:]
            a_buf[slot + j, pl.ds(SIDE, 1), :] = a_bot[pl.ds(z + j, 1), :]
            b_buf[slot + j, pl.ds(SIDE, 1), :] = b_bot[pl.ds(z + j, 1), :]

    def rows_of(j, y0):
        a = a_buf[j, pl.ds(y0, 16), :]
        b = b_buf[j, pl.ds(y0, 16), :]
        dy = a_buf[j, pl.ds(y0 + 1, 16), :] - a
        along_xy = a + ty * dy
        diff_xy = b + ty * (b_buf[j, pl.ds(y0 + 1, 16), :] - b)
        return along_xy, diff_xy, dy

    def compute(k):
        def tile(t, carry):
            y0 = pl.multiple_of(t * 16, 16)
            w1, x1, y1 = rows_of(S, y0)
            sums = [[jnp.zeros((16, SIDE), F32) for _ in range(4)] for _ in range(3)]
            for j in reversed(range(S)):
                w0, x0, yy0 = rows_of(j, y0)
                gz = w1 - w0
                res = w0 + tz * gz - fixed[k * S + j, pl.ds(y0, 16), :].astype(F32)
                grads = (x0 + tz * (x1 - x0), yy0 + tz * (y1 - yy0), gz)
                for d in range(3):
                    value = res * grads[d]
                    for m in range(4):
                        value = sums[d][m] + value
                        sums[d][m] = value
                w1, x1, y1 = w0, x0, yy0
            for d in range(3):
                for m in range(4):
                    high, low = split(sums[d][m])
                    place = pl.ds(pl.multiple_of(d * SIDE + y0, 16), 16)
                    mom[place, pl.ds(m * 256, 128)] = high
                    mom[place, pl.ds(m * 256 + 128, 128)] = low
            return carry

        lax.fori_loop(0, SIDE // 16, tile, 0)
        a_buf[S] = a_buf[0]
        b_buf[S] = b_buf[0]

        parts = mm(mom[...], rhs_x[...])
        parts = parts[:, :SIDE] + parts[:, SIDE:]
        wide = jnp.concatenate([parts[d * SIDE:(d + 1) * SIDE] for d in range(3)], axis=1)
        high, low = split(wide)
        h_x[pl.ds(0, SIDE), :] = high
        h_x[pl.ds(SIDE, SIDE), :] = low
        both_y = mm(lhs_y[...], h_x[...])
        rough = both_y[64:80] + both_y[80:96]
        rough = jnp.concatenate([rough[:, d * SIDE:(d + 1) * SIDE] for d in range(3)], axis=0)
        high, low = split(rough)
        weights = w_c[k]
        coarse[...] += mm(high, weights) + mm(low, weights)
        done = both_y[:32] + both_y[32:64]
        turn = lax.rem(k + 3, 4)
        base = (k + 3) // 4
        blocks = iota((32, SIDE), 1) // 32
        for d in range(3):
            moved = pltpu.roll(done[:, d * SIDE:(d + 1) * SIDE], turn * 32, 1)
            place = pl.ds(d * SIDE, SIDE)
            acc[base, :, place] += jnp.where(blocks >= turn, moved, 0.0)
            acc[base + 1, :, place] += jnp.where(blocks < turn, moved, 0.0)

    def step(n, carry):
        k = 7 - n

        @pl.when(jnp.logical_and(k >= 3, jnp.logical_not(row3)))
        def _():
            for h in (1, 0):
                s1(part(k - 3, h)).start()

        for h in (1, 0):
            @pl.when(k >= 1)
            def _(h=h):
                forward(part(k - 1, h), HALF, k - 1, h)

            if h == 1:
                @pl.when(k == 7)
                def _():
                    forward(last, 1)
                    landing(last)
                    lerp_x(DEPTH, S, 1)

            landing(part(k, h))
            lerp_x(k * S + h * HALF, h * HALF, HALF)
        compute(k)

        @pl.when(k == 6)
        def _():
            top_out[...] = acc[3]

            @pl.when(above)
            def _():
                up_z.start()

        return carry

    lax.fori_loop(0, CELLS, step, 0)

    c_z[l] = coarse[...]
    z_turns = (2, 1, 3)
    z_copies = [
        remote(c_z.at[l], c_z.at[l], cz_s.at[o], cz_r.at[l], (g, r, lax.rem(l + o, GZ))) for o in z_turns
    ]
    for copy in z_copies:
        copy.start()

    blocks = iota((32, SIDE), 1) // 32
    packed = jnp.zeros((32, SIDE), F32)
    for d in range(3):
        packed += jnp.where(
            blocks == d, pltpu.roll(acc[0, :, pl.ds(d * SIDE, SIDE)], 32 * (d + 1), 1), 0.0
        )
    low_out[...] = packed
    down_z = remote(low_out, low_in, fine_s.at[1], fine_r.at[1], low_slab)

    @pl.when(below)
    def _():
        down_z.start()

    fold[...] = acc[pl.ds(1, 2)]

    def weigh(block, weights, at):
        high, low = split(block)
        rows = block.shape[0]
        pair = mm(jnp.concatenate([high, low], axis=0), weights[0, at, :])
        return pair[:rows] + pair[rows:] + mm(high, weights[1, at, :])

    def span(dev):
        return pl.ds(pl.multiple_of(dev * SIDE, SIDE), SIDE)

    total = weigh(coarse[...], w_z, span(l))
    for o in (1, 3, 2):
        dev = lax.rem(l + o, GZ)
        remote(c_z.at[dev], c_z.at[dev], cz_s.at[o], cz_r.at[dev], partner).wait_recv()
        total += weigh(c_z[dev], w_z, span(dev))
    c_y[r] = total
    y_copies = [
        remote(c_y.at[r], c_y.at[r], cy_s.at[o], cy_r.at[r], (g, lax.rem(r + o, GY), l)) for o in (2, 1, 3)
    ]
    for copy in y_copies:
        copy.start()

    @pl.when(below)
    def _():
        up_z.wait_recv()
        fold[0] += top_in[...]

    @pl.when(above)
    def _():
        down_z.wait_recv()
        for d in range(3):
            turned = pltpu.roll(low_in[...], SIDE - 32 * (d + 1), 1)
            fold[1, :, pl.ds(d * SIDE, SIDE)] += jnp.where(blocks == 3, turned, 0.0)

    up_y = remote(fold.at[:, pl.ds(24, 8)], f_y.at[0], fine_s.at[2], fine_r.at[2], high_row)
    down_y = remote(fold.at[:, pl.ds(0, 8)], f_y.at[1], fine_s.at[3], fine_r.at[3], low_row)

    @pl.when(has_high)
    def _():
        up_y.start()

    @pl.when(has_low)
    def _():
        down_y.start()

    for o in (1, 3, 2):
        dev = lax.rem(r + o, GY)
        remote(c_y.at[dev], c_y.at[dev], cy_s.at[o], cy_r.at[dev], partner).wait_recv()
    gathered = jnp.concatenate(
        [
            jnp.concatenate([c_y[dev, pl.ds(d * 16, 16), :] for d in range(3)], axis=1)
            for dev in range(GY)
        ],
        axis=0,
    )
    high, low = split(gathered)
    both_y = mm(m_y[...], jnp.concatenate([high, low], axis=0))
    both_y = both_y[:16] + both_y[16:]
    both_y = jnp.concatenate([both_y[:, d * SIDE:(d + 1) * SIDE] for d in range(3)], axis=0)
    c_x[g] = both_y

    x_turns = [(2, 1), (1, 1), (3, 1), (2, 0), (0, 1), (1, 0), (3, 0)]

    def other(turn):
        dz, dx = turn
        return 2 * lax.rem(g // 2 + dz, GX // 2) + lax.rem(lax.rem(g, 2) + dx, 2)

    x_copies = [
        remote(c_x.at[g], c_x.at[g], cx_s.at[i], cx_r.at[g], (other(turn), r, l))
        for i, turn in enumerate(x_turns)
    ]
    for copy in x_copies:
        copy.start()

    @pl.when(has_low)
    def _():
        up_y.wait_recv()
        fold[:, pl.ds(8, 8), :] += f_y[0]

    @pl.when(has_high)
    def _():
        down_y.wait_recv()
        fold[:, pl.ds(16, 8), :] += f_y[1]

    spot = lax.rem(iota((16, SIDE), 1), 32)
    parts = [
        fold[half, pl.ds(8, 16), pl.ds(d * SIDE, SIDE)] for half in range(2) for d in range(3)
    ]
    to_right, to_left = jnp.zeros((16, SIDE), F32), jnp.zeros((16, SIDE), F32)
    for n, value in enumerate(parts):
        ends = jnp.where(jnp.logical_or(spot == 24, spot == 25), value, 0.0)
        to_right += ends if n == 0 else pltpu.roll(ends, 2 * n, 1)
        ends = jnp.where(spot == 7, value, 0.0)
        to_left += ends if n == 0 else pltpu.roll(ends, n, 1)
    x_out[0] = to_right
    x_out[1] = to_left
    up_x = remote(x_out.at[0], x_in.at[0], fine_s.at[4], fine_r.at[4], right)
    down_x = remote(x_out.at[1], x_in.at[1], fine_s.at[5], fine_r.at[5], left)

    @pl.when(has_next)
    def _():
        up_x.start()

    @pl.when(has_prev)
    def _():
        down_x.start()

    @pl.when(jnp.logical_not(has_prev))
    def _():
        x_in[0] = jnp.zeros((16, SIDE), F32)

    @pl.when(jnp.logical_not(has_next))
    def _():
        x_in[1] = jnp.zeros((16, SIDE), F32)

    corr = weigh(both_y, w_x, span(g))

    def take(i):
        dev = other(x_turns[i])
        remote(c_x.at[dev], c_x.at[dev], cx_s.at[i], cx_r.at[dev], partner).wait_recv()
        return weigh(c_x[dev], w_x, span(dev))

    for i in (6, 5, 4, 3):
        corr += take(i)

    @pl.when(has_prev)
    def _():
        up_x.wait_recv()

    @pl.when(has_next)
    def _():
        down_x.wait_recv()

    from_left, from_right = x_in[0], x_in[1]
    fine = []
    for n, value in enumerate(parts):
        before = pltpu.roll(from_left, SIDE - 16 - 2 * n, 1)
        after = pltpu.roll(from_right, 16 - n, 1)
        value = value + jnp.where(jnp.logical_or(spot == 8, spot == 9), before, 0.0)
        fine.append(value + jnp.where(spot == 23, after, 0.0))

    for i in (2, 1, 0):
        corr += take(i)
    for half in range(2):
        for d in range(3):
            value = fine[half * 3 + d] + corr[d * 16:(d + 1) * 16, half * SIDE:(half + 1) * SIDE]
            for b in range(4):
                out[d, half * 4 + b] = value[:, b * 32 + 8:b * 32 + 24]

    @pl.when(below)
    def _():
        plane.wait_send()
        down_z.wait_send()

    @pl.when(above)
    def _():
        up_z.wait_send()

    @pl.when(has_low)
    def _():
        own_low.wait_send()
        x_low.wait_send()
        down_y.wait_send()

    @pl.when(has_high)
    def _():
        own_high.wait_send()
        x_high.wait_send()
        up_y.wait_send()

    @pl.when(has_prev)
    def _():
        t_left.wait_send()
        down_x.wait_send()

    @pl.when(has_next)
    def _():
        s_right.wait_send()
        up_x.wait_send()

    @pl.when(row2)
    def _():
        flag_up.wait_send()

    @pl.when(asks_left)
    def _():
        flag_left.wait_send()

    for copy in z_copies + y_copies + x_copies:
        copy.wait_send()

    def drain(piece):
        h2(relay, piece).wait_send()

        @pl.when(jnp.logical_not(row3))
        def _():
            s1(piece).wait_send()

        @pl.when(has_next)
        def _():
            h1(piece).wait_send()

        @pl.when(either(row0, row3))
        def _():
            s2(relay, piece).wait_send()

    drain(last)

    def drain_cell(k, carry):
        for h in (1, 0):
            drain(part(k, h))
        return carry

    lax.fori_loop(0, CELLS, drain_cell, 0)


def per_device(
    fixed_image, moving_image, block_shift, fraction, brick_valid, precond_x, precond_y, precond_z
):
    dma = pltpu.SemaphoreType.DMA
    vmem = pltpu.VMEM
    brick = vmem((DEPTH + 1, SIDE, SIDE), BF16)
    hbm_spec = pl.BlockSpec(memory_space=pltpu.HBM)
    smem = pltpu.SMEM
    vmem_spec = pl.BlockSpec(memory_space=pltpu.VMEM)
    return pl.pallas_call(
        kernel,
        out_shape=jax.ShapeDtypeStruct((3, 8, 16, 16), F32),
        in_specs=[hbm_spec] * 8,
        out_specs=vmem_spec,
        scratch_shapes=[
            smem((2,), jnp.int32), smem((3,), jnp.int32), smem((1, 1, 1), jnp.int32),
            vmem((64, 64), F32), vmem((32, 32), F32), vmem((16, 16), F32),
            brick, brick, brick, brick, brick, brick,
            vmem((DEPTH, SIDE, SIDE), BF16),
            vmem((SIDE, SIDE), BF16), vmem((SIDE, SIDE), BF16),
            vmem((160, SIDE), BF16), vmem((160, SIDE), BF16), vmem((160, SIDE), BF16),
            vmem((160, SIDE), BF16), vmem((80, SIDE), BF16), vmem((80, SIDE), BF16),
            vmem((SIDE, SIDE), F32), vmem((80, SIDE), F32), vmem((80, SIDE), F32),
            vmem((S * SIDE, 256), BF16), vmem((256, 256), BF16),
            vmem((S + 1, SIDE + 8, SIDE), F32), vmem((S + 1, SIDE + 8, SIDE), F32),
            vmem((3 * SIDE, 1024), BF16), vmem((1024, 256), BF16), vmem((96, 256), BF16),
            vmem((4, 32, 384), F32), vmem((48, SIDE), F32), vmem((CELLS, SIDE, SIDE), BF16),
            vmem((2, 512, SIDE), BF16), vmem((2, 1024, 256), BF16), vmem((32, SIDE), BF16),
            vmem((GZ, 48, SIDE), F32), vmem((GY, 48, SIDE), F32), vmem((GX, 48, SIDE), F32),
            vmem((32, 384), F32), vmem((32, 384), F32), vmem((32, SIDE), F32), vmem((32, SIDE), F32),
            vmem((2, 2, 8, 384), F32), vmem((2, 16, SIDE), F32), vmem((2, 16, SIDE), F32),
            vmem((2, 32, 384), F32), vmem((256, 384), BF16),
            dma((8,)),
            *[dma((PIECES,))] * 8,
            dma((8,)), dma((8,)), dma((6,)), dma((6,)),
            dma((GZ,)), dma((GZ,)), dma((GY,)), dma((GY,)), dma((GX,)), dma((GX,)),
        ],
        compiler_params=pltpu.CompilerParams(
            collective_id=0, has_side_effects=True, vmem_limit_bytes=60 * 2**20
        ),
        name="registration_gradient",
    )(
        moving_image, fixed_image, block_shift.reshape(2), fraction.reshape(3),
        brick_valid, precond_x, precond_y, precond_z,
    )


def solution(mesh):
    return jax.shard_map(
        per_device,
        mesh=mesh,
        in_specs=(
            P("gz", "gy", "gx"),
            P("gz", "gy", "gx"),
            P(None, "gz", "gy", "gx"),
            P(None, "gz", "gy", "gx"),
            P("gz", "gy", "gx"),
            P(),
            P(),
            P(),
        ),
        out_specs=P(None, "gz", "gy", "gx"),
        check_vma=False,
    )
```

```python
import jax
import jax.numpy as jnp
import numpy as np
from jax import lax
from jax.experimental import pallas as pl
from jax.experimental.pallas import tpu as pltpu
from jax.sharding import PartitionSpec as P

S = 8
SIDE = 128
DEPTH = 64
CELLS = DEPTH // S
HALF = S // 2
PIECES = 2 * CELLS
GX, GY, GZ = 8, 4, 4
FULL = lax.Precision.HIGHEST
F32 = jnp.float32
BF16 = jnp.bfloat16
MESH = pl.DeviceIdType.MESH


def tap_polynomials():
    j = np.arange(S, dtype=np.float64)
    basis = np.stack(
        [np.ones(S), j + 1, (j + 1) * (j + 2) / 2, (j + 1) * (j + 2) * (j + 3) / 6], axis=1
    )
    taps = []
    for a in range(4):
        u = np.abs(j / S - (a - 1))
        taps.append(
            np.where(u < 1, 2 / 3 - u**2 + u**3 / 2, np.where(u < 2, (2 - u) ** 3 / 6, 0.0))
        )
    return np.linalg.lstsq(basis, np.stack(taps, axis=1), rcond=None)[0]


TAPS = tap_polynomials()


def iota(shape, dim):
    return lax.broadcasted_iota(jnp.int32, shape, dim)


def spline(distance):
    dist = jnp.abs(distance)
    inner = 2.0 / 3.0 - dist * dist + dist * dist * dist / 2.0
    far = 2.0 - dist
    outer = far * far * far / 6.0
    return jnp.where(dist < 1.0, inner, jnp.where(dist < 2.0, outer, 0.0))


def weight(gap):
    gap = jnp.abs(gap)
    return jnp.where(gap == 0, 0.75, jnp.where(gap == 1, 0.5, jnp.where(gap == 2, 0.125, 0.0)))


def split(value):
    high = value.astype(BF16)
    return high, (value - high.astype(F32)).astype(BF16)


def mm(a, b):
    return jnp.dot(a, b, preferred_element_type=F32)


def mm_full(a, b, dims=((1,), (0,))):
    return lax.dot_general(a, b, (dims, ((), ())), precision=FULL, preferred_element_type=F32)


def kernel(
    mov, fix, shift_h, frac_h, valid_h, px_h, py_h, pz_h, out,
    shift, frac, valid, px, py, pz,
    own, relay, land, stage, sib1, sib2, fixed,
    flag_out, flag_in, e_own, e_x, e_up, e_up_x, e_down, e_down_x, t_sel, a_bot, b_bot,
    lhs, rhs, a_buf, b_buf, mom, rhs_x, lhs_y, acc, coarse, w_c,
    w_z, w_x, m_y, c_z, c_y, c_x, c_out, top_out, top_in, low_out, low_in, f_y, x_out, x_in, fold, h_x,
    local_sem, h1_s, h1_r, h2_s, h2_r, s1_s, s1_r, s2_s, s2_r,
    edge_s, edge_r, fine_s, fine_r, cz_s, cz_r, cy_s, cy_r, cx_s, cx_r,
):
    g, r, l = lax.axis_index("gx"), lax.axis_index("gy"), lax.axis_index("gz")
    across = lax.rem(r + 2, GY)
    sibling = (g, r + 1 - 2 * lax.rem(r, 2), l)
    partner = (g, across, l)

    def remote(src, dst, send, recv, device):
        return pltpu.make_async_remote_copy(
            src_ref=src, dst_ref=dst, send_sem=send, recv_sem=recv,
            device_id=device, device_id_type=MESH,
        )

    smalls = [
        pltpu.make_async_copy(src, dst, local_sem.at[2 + i])
        for i, (src, dst) in enumerate(
            ((shift_h, shift), (frac_h, frac), (valid_h, valid), (px_h, px), (py_h, py), (pz_h, pz))
        )
    ]
    for copy in smalls:
        copy.start()
    load_own = pltpu.make_async_copy(mov, own.at[pl.ds(0, DEPTH)], local_sem.at[0])
    load_fixed = pltpu.make_async_copy(fix, fixed, local_sem.at[1])
    load_own.start()
    load_fixed.start()

    peers = [(lax.rem(g + o, GX), r, l) for o in (1, 2, 4, 6, 7)]
    peers += [(g, lax.rem(r + o, GY), l) for o in range(1, GY)]
    peers += [(g, r, lax.rem(l + o, GZ)) for o in range(1, GZ)]
    peers += [(lax.rem(g + o, GX), across, l) for o in (1, GX - 1)]
    mate = g + 1 - 2 * lax.rem(g, 2)
    peers += [(mate, lax.rem(r + o, GY), l) for o in range(GY)]
    barrier = pltpu.get_barrier_semaphore()
    for peer in peers:
        pl.semaphore_signal(barrier, inc=1, device_id=peer, device_id_type=MESH)
    for copy in smalls:
        copy.wait()
    ox, oy = shift[0], shift[1]
    tx = frac[0].astype(F32) / 64.0
    ty = frac[1].astype(F32) / 64.0
    tz = frac[2].astype(F32) / 64.0
    live = valid[0, 0, 0].astype(F32)
    flag_out[...] = jnp.full((8, SIDE), -oy.astype(F32), F32)
    pl.semaphore_wait(barrier, len(peers))

    def part(k, h):
        if isinstance(k, int):
            return pl.ds(k * S + h * HALF, HALF + (k == CELLS - 1 and h == 1)), 2 * k + h
        return pl.ds(pl.multiple_of(k * S + h * HALF, HALF), HALF), 2 * k + h

    def source(piece):
        return own if piece[0].size > HALF else mov

    def h1(piece, src=None):
        sl, i = piece
        if src is None:
            src = source(piece)
        return remote(
            src.at[sl], relay.at[sl], h1_s.at[i], h1_r.at[i], (lax.rem(g + 1, GX), across, l)
        )

    def h2(src, piece):
        sl, i = piece
        return remote(src.at[sl], land.at[sl], h2_s.at[i], h2_r.at[i], partner)

    def s1(piece):
        sl, i = piece
        return remote(source(piece).at[sl], sib1.at[sl], s1_s.at[i], s1_r.at[i], sibling)

    def s2(src, piece):
        sl, i = piece
        return remote(src.at[sl], sib2.at[sl], s2_s.at[i], s2_r.at[i], sibling)

    has_next, has_prev = g < GX - 1, g > 0
    above, below = l < GZ - 1, l > 0
    has_low, has_high = r > 0, r < GY - 1
    row0, row1, row2, row3 = (r == i for i in range(4))
    either = jnp.logical_or

    left = (lax.rem(g + GX - 1, GX), r, l)
    right = (lax.rem(g + 1, GX), r, l)
    low_row = (g, lax.rem(r + GY - 1, GY), l)
    high_row = (g, lax.rem(r + 1, GY), l)
    low_slab = (g, r, lax.rem(l + GZ - 1, GZ))
    high_slab = (g, r, lax.rem(l + 1, GZ))

    plane = remote(mov.at[pl.ds(0, 1)], own.at[pl.ds(DEPTH, 1)], edge_s.at[6], edge_r.at[6], low_slab)
    flag_up = remote(flag_out, flag_in, edge_s.at[7], edge_r.at[7], partner)
    flag_left = remote(flag_out, flag_in, edge_s.at[7], edge_r.at[7], left)
    asks_left = jnp.logical_and(row3, has_prev)
    asked = jnp.logical_and(row3, has_next)

    def early(k):
        @pl.when(jnp.logical_and(has_next, jnp.logical_not(row3)))
        def _():
            h1(part(k, 0)).start()

    early(7)

    @pl.when(below)
    def _():
        plane.start()

    @pl.when(row2)
    def _():
        flag_up.start()

    @pl.when(asks_left)
    def _():
        flag_left.start()

    @pl.when(jnp.logical_not(row3))
    def _():
        s1(part(7, 0)).start()
        s1(part(6, 0)).start()

    early(6)

    def blend(first, second, sl):
        flagged = jnp.max(flag_in[...]) > 0.5
        for j in range(sl.size):
            z = sl.start + j
            stage[z] = jnp.where(flagged, first[z], second[z])

    def send(piece):
        @pl.when(jnp.logical_and(has_next, jnp.logical_not(row3)))
        def _():
            h1(piece).start()

        @pl.when(row3)
        def _():
            s1(piece).wait_recv()

        @pl.when(asked)
        def _():
            blend(sib1, own, piece[0])
            h1(piece, stage).start()

    zero_plane = jnp.zeros((1, SIDE, SIDE), BF16)

    @pl.when(jnp.logical_not(above))
    def _():
        own[pl.ds(DEPTH, 1)] = zero_plane

    @pl.when(jnp.logical_not(has_prev))
    def _():
        def clear(z, carry):
            relay[pl.ds(z, 1)] = zero_plane
            return carry

        lax.fori_loop(0, DEPTH + 1, clear, 0)

    lane = iota((SIDE, SIDE), 1)
    row = iota((SIDE, SIDE), 0)

    rhs_lane = iota((2 * SIDE, 2 * SIDE), 1)
    rhs_row = iota((2 * SIDE, 2 * SIDE), 0)
    col = lax.rem(rhs_lane, SIDE)
    is_lerp = rhs_lane < SIDE
    here = jnp.where(is_lerp, 1.0 - tx, -1.0)
    there = jnp.where(is_lerp, tx, 1.0)
    top = jnp.where(rhs_row == col, here, jnp.where(rhs_row == col + 1, there, 0.0))
    rhs[...] = jnp.where(
        rhs_row < SIDE, top, jnp.where(col == SIDE - 1, there, 0.0)
    ).astype(BF16)

    point = lax.rem(lane, 32) - 8
    tap = lane // 32
    px_ok = jnp.logical_and(g * 16 + point >= 0, g * 16 + point < 16 * GX)
    basis_x = jnp.where(px_ok, spline(row.astype(F32) / S - point.astype(F32)), 0.0)
    for m in range(4):
        scale = jnp.full((SIDE, SIDE), float(TAPS[m, 3]), F32)
        for a in (2, 1, 0):
            scale = jnp.where(tap == a, float(TAPS[m, a]), scale)
        high, low = split(basis_x * scale)
        for half in range(2):
            rhs_x[pl.ds(m * 256 + half * 128, 128), pl.ds(0, 128)] = high
            rhs_x[pl.ds(m * 256 + half * 128, 128), pl.ds(128, 128)] = low

    q_point = iota((32, SIDE), 0) - 8
    q_ok = jnp.logical_and(r * 16 + q_point >= 0, r * 16 + q_point < 16 * GY)
    basis_y = jnp.where(
        q_ok, spline(iota((32, SIDE), 1).astype(F32) / S - q_point.astype(F32)), 0.0
    ) * (live * S ** (-1.5))
    high, low = split(basis_y)
    lhs_y[pl.ds(0, 32), pl.ds(0, 128)] = high
    lhs_y[pl.ds(0, 32), pl.ds(128, 128)] = high
    lhs_y[pl.ds(32, 32), pl.ds(0, 128)] = low
    lhs_y[pl.ds(32, 32), pl.ds(128, 128)] = jnp.zeros((32, SIDE), BF16)

    coarse_y = mm_full(weight(iota((16, 32), 1) - 8 - 2 * (iota((16, 32), 0) - 1)), basis_y)
    high, low = split(coarse_y)
    lhs_y[pl.ds(64, 16), pl.ds(0, 128)] = high
    lhs_y[pl.ds(64, 16), pl.ds(128, 128)] = high
    lhs_y[pl.ds(80, 16), pl.ds(0, 128)] = low
    lhs_y[pl.ds(80, 16), pl.ds(128, 128)] = jnp.zeros((16, SIDE), BF16)

    def cell_weights(k, carry):
        z_point = k + row // 32 - 1
        z_ok = jnp.logical_and(l * 8 + z_point >= 0, l * 8 + z_point < 8 * GZ)
        both_w = weight(z_point - 2 * (lane // 16 - 1)) * weight(
            lax.rem(row, 32) - 8 - 2 * (lax.rem(lane, 16) - 1)
        )
        w_c[k] = jnp.where(z_ok, both_w, 0.0).astype(BF16)
        return carry

    lax.fori_loop(0, CELLS, cell_weights, 0)
    coarse[...] = jnp.zeros((48, SIDE), F32)
    wr, wl = iota((512, SIDE), 0), iota((512, SIDE), 1)

    load_own.wait()

    @pl.when(asked)
    def _():
        flag_left.wait_recv()

    @pl.when(row3)
    def _():
        send(part(7, 0))
        send(part(6, 0))

    @pl.when(above)
    def _():
        plane.wait_recv()

    @pl.when(jnp.logical_not(row3))
    def _():
        for k, h in ((7, 1), (6, 1), (5, 0), (5, 1)):
            s1(part(k, h)).start()

    send(part(7, 1))

    kz = 4 * (iota((512, 16), 0) // 128) + lax.rem(iota((512, 16), 0) // 16, 8) - 1
    pick_z = (kz == iota((512, 16), 1)).astype(F32)
    spread_z = weight(l * 8 + iota((16, SIDE), 1) // 16 - 2 * iota((16, SIDE), 0))
    full_z = mm_full(mm_full(pick_z, pz[...], ((1,), (1,))), spread_z)
    full_z = jnp.where(lax.rem(wr, 16) == lax.rem(wl, 16), full_z, 0.0)
    high, low = split(full_z)
    w_z[0], w_z[1] = high, low

    jy = 8 * (iota((32, 64), 1) // 16) + lax.rem(iota((32, 64), 1), 16) - 1
    pick_y = (jy == iota((32, 64), 0)).astype(F32)
    spread_y = weight(r * 16 + iota((16, 32), 0) - 2 * iota((16, 32), 1))
    full_y = mm_full(spread_y, mm_full(py[...], pick_y))
    high, low = split(full_y)
    m_y[...] = jnp.concatenate(
        [
            jnp.concatenate([high.astype(F32), high.astype(F32)], axis=1),
            jnp.concatenate([low.astype(F32), jnp.zeros((16, 64), F32)], axis=1),
        ],
        axis=0,
    ).astype(BF16)

    xl = iota((64, 512), 1)
    spread_x = weight(16 * (2 * (xl // 128) + lax.rem(g, 2)) + lax.rem(xl, 16) - 2 * iota((64, 512), 0))
    kx = 8 * (g - lax.rem(g, 2) + iota((256, 64), 0) // 128) + lax.rem(iota((256, 64), 0), 16) - 1
    pick_x = (kx == iota((256, 64), 1)).astype(F32)
    full_x = mm_full(pick_x, mm_full(px[...], spread_x, ((0,), (0,))))
    same = lax.rem(iota((256, 512), 0) // 16, 8) == lax.rem(iota((256, 512), 1) // 16, 8)
    high, low = split(jnp.where(same, full_x, 0.0))
    w_x[0], w_x[1] = high, low

    def clear_acc(i, carry):
        acc[i] = jnp.zeros((32, 384), F32)
        return carry

    lax.fori_loop(0, 4, clear_acc, 0)

    moved_x, moved_y = ox != 0, oy != 0
    both = jnp.logical_and(moved_x, moved_y)

    use_own = jnp.logical_not(jnp.logical_or(moved_x, moved_y))
    only_x = jnp.logical_and(moved_x, jnp.logical_not(moved_y))
    only_y = jnp.logical_and(moved_y, jnp.logical_not(moved_x))
    use_land = either(
        only_x, either(jnp.logical_and(row2, only_y), jnp.logical_and(row3, both))
    )
    use_sib1 = jnp.logical_and(either(row1, row3), only_y)
    use_sib2 = jnp.logical_and(either(row1, row2), both)

    def choose(z):
        value = jnp.where(use_sib2, sib2[z], jnp.zeros((SIDE, SIDE), BF16))
        value = jnp.where(use_sib1, sib1[z], value)
        value = jnp.where(use_land, land[z], value)
        return jnp.where(use_own, own[z], value)

    def forward(k, h):
        piece = part(k, h)

        @pl.when(has_prev)
        def _():
            h1(piece).wait_recv()

        @pl.when(row0)
        def _():
            s1(piece).wait_recv()
            blend(sib1, relay, piece[0])
            h2(stage, piece).start()

        @pl.when(jnp.logical_not(row0))
        def _():
            h2(relay, piece).start()

        if isinstance(k, int) and k >= 6:
            send(part(*{(7, 0): (6, 1), (6, 0): (5, 0), (7, 1): (5, 1), (6, 1): (4, 0)}[k, h]))
        else:
            @pl.when(k >= 1 + h)
            def _():
                send(part(k - 1 - h, 1 - h))

        @pl.when(row3)
        def _():
            s2(relay, piece).start()

    def landing(piece):
        h2(relay, piece).wait_recv()

        @pl.when(row0)
        def _():
            s2(land, piece).start()

        @pl.when(row1)
        def _():
            s1(piece).wait_recv()

        @pl.when(either(row1, row2))
        def _():
            s2(relay, piece).wait_recv()

    def more(k):
        @pl.when(jnp.logical_not(row3))
        def _():
            for h in (0, 1):
                s1(part(k, h)).start()

    up_z = remote(top_out, top_in, fine_s.at[0], fine_r.at[0], high_slab)

    @pl.when(row0)
    def _():
        flag_up.wait_recv()

    forward(7, 0)
    def edge_step(z, carry):
        t, s = carry
        value = own[z].astype(F32)
        t = jnp.where(lane == z, jnp.broadcast_to(value[:, 0:1], (SIDE, SIDE)), t)
        s = jnp.where(row[:80] == z, jnp.broadcast_to(value[0:1, :], (80, SIDE)), s)
        return t, s

    t_own, s_own = lax.fori_loop(
        0, DEPTH, edge_step, (jnp.zeros((SIDE, SIDE), F32), jnp.zeros((80, SIDE), F32))
    )

    t_own, s_own = edge_step(DEPTH, (t_own, s_own))
    rows_s, rows_t = pl.ds(0, 80), pl.ds(80, 80)
    e_own[rows_s, :] = s_own.astype(BF16)
    e_own[rows_t, :] = jnp.transpose(t_own)[:80].astype(BF16)

    s_right = remote(e_own.at[rows_s], e_x.at[rows_s], edge_s.at[0], edge_r.at[0], right)
    t_left = remote(e_own.at[rows_t], e_x.at[rows_t], edge_s.at[1], edge_r.at[1], left)
    own_low = remote(e_own.at[rows_s], e_up, edge_s.at[2], edge_r.at[2], low_row)
    x_low = remote(e_x, e_up_x, edge_s.at[3], edge_r.at[3], low_row)
    own_high = remote(e_own.at[rows_t], e_down, edge_s.at[4], edge_r.at[4], high_row)
    x_high = remote(e_x.at[rows_t], e_down_x, edge_s.at[5], edge_r.at[5], high_row)

    @pl.when(has_next)
    def _():
        s_right.start()

    @pl.when(has_prev)
    def _():
        t_left.start()

    @pl.when(has_low)
    def _():
        own_low.start()

    @pl.when(has_high)
    def _():
        own_high.start()

    forward(6, 0)
    forward(7, 1)
    def arrive(copy, dst, ok):
        @pl.when(ok)
        def _():
            copy.wait_recv()

        @pl.when(jnp.logical_not(ok))
        def _():
            dst[...] = jnp.zeros(dst.shape, BF16)

    arrive(s_right, e_x.at[rows_s], has_prev)
    arrive(t_left, e_x.at[rows_t], has_next)

    @pl.when(has_low)
    def _():
        x_low.start()

    @pl.when(has_high)
    def _():
        x_high.start()

    more(4)
    forward(6, 1)
    arrive(own_low, e_up, has_high)
    arrive(own_high, e_down, has_low)
    arrive(x_low, e_up_x, has_high)
    arrive(x_high, e_down_x, has_low)

    def pick(stay, by_x, by_y, by_both):
        return jnp.where(moved_y, jnp.where(moved_x, by_both, by_y), jnp.where(moved_x, by_x, stay))

    def wide(ref, rows):
        return ref[rows, :].astype(F32)

    t_here, t_right = wide(e_own, rows_t), wide(e_x, rows_t)
    t_wide = pick(t_right, t_here, e_down_x[...].astype(F32), e_down[...].astype(F32))
    t_sel[...] = jnp.transpose(jnp.concatenate([t_wide, jnp.zeros((48, SIDE), F32)], axis=0))
    s_sel = pick(e_up[...].astype(F32), wide(e_up_x, rows_s), wide(e_own, rows_s), wide(e_x, rows_s))
    k_sel = pick(wide(e_up_x, rows_t), e_up[...].astype(F32), t_right, t_here)
    diag = jnp.where(lane[:80] == row[:80], jnp.broadcast_to(k_sel[:, 0:1], (80, SIDE)), 0.0)
    bottom = mm(jnp.concatenate([s_sel, diag], axis=1).astype(BF16), rhs[...])
    a_bot[...] = bottom[:, :SIDE]
    b_bot[...] = bottom[:, SIDE:]


    load_fixed.wait()

    def fill(z, j):
        lhs[pl.ds(j * SIDE, SIDE), pl.ds(0, SIDE)] = choose(z)
        lhs[pl.ds(j * SIDE, SIDE), pl.ds(SIDE, SIDE)] = jnp.where(lane == z, t_sel[...], 0.0).astype(BF16)

    def lerp_x(z, slot, count):
        for j in range(count):
            fill(z + j, j)
        both_x = mm(lhs[pl.ds(0, count * SIDE), :], rhs[...])
        for j in range(count):
            rows = slice(j * SIDE, (j + 1) * SIDE)
            a_buf[slot + j, pl.ds(0, SIDE), :] = both_x[rows, :SIDE]
            b_buf[slot + j, pl.ds(0, SIDE), :] = both_x[rows, SIDE:]
            a_buf[slot + j, pl.ds(SIDE, 1), :] = a_bot[pl.ds(z + j, 1), :]
            b_buf[slot + j, pl.ds(SIDE, 1), :] = b_bot[pl.ds(z + j, 1), :]

    def rows_of(j, y0):
        a = a_buf[j, pl.ds(y0, 16), :]
        b = b_buf[j, pl.ds(y0, 16), :]
        dy = a_buf[j, pl.ds(y0 + 1, 16), :] - a
        along_xy = a + ty * dy
        diff_xy = b + ty * (b_buf[j, pl.ds(y0 + 1, 16), :] - b)
        return along_xy, diff_xy, dy

    def compute(k):
        def tile(t, carry):
            y0 = pl.multiple_of(t * 16, 16)
            w1, x1, y1 = rows_of(S, y0)
            sums = [[jnp.zeros((16, SIDE), F32) for _ in range(4)] for _ in range(3)]
            for j in reversed(range(S)):
                w0, x0, yy0 = rows_of(j, y0)
                gz = w1 - w0
                res = w0 + tz * gz - fixed[k * S + j, pl.ds(y0, 16), :].astype(F32)
                grads = (x0 + tz * (x1 - x0), yy0 + tz * (y1 - yy0), gz)
                for d in range(3):
                    value = res * grads[d]
                    for m in range(4):
                        value = sums[d][m] + value
                        sums[d][m] = value
                w1, x1, y1 = w0, x0, yy0
            for d in range(3):
                for m in range(4):
                    high, low = split(sums[d][m])
                    place = pl.ds(pl.multiple_of(d * SIDE + y0, 16), 16)
                    mom[place, pl.ds(m * 256, 128)] = high
                    mom[place, pl.ds(m * 256 + 128, 128)] = low
            return carry

        lax.fori_loop(0, SIDE // 16, tile, 0)
        a_buf[S] = a_buf[0]
        b_buf[S] = b_buf[0]

        parts = mm(mom[...], rhs_x[...])
        parts = parts[:, :SIDE] + parts[:, SIDE:]
        wide = jnp.concatenate([parts[d * SIDE:(d + 1) * SIDE] for d in range(3)], axis=1)
        high, low = split(wide)
        h_x[pl.ds(0, SIDE), :] = high
        h_x[pl.ds(SIDE, SIDE), :] = low
        both_y = mm(lhs_y[...], h_x[...])
        rough = both_y[64:80] + both_y[80:96]
        rough = jnp.concatenate([rough[:, d * SIDE:(d + 1) * SIDE] for d in range(3)], axis=0)
        high, low = split(rough)
        weights = w_c[k]
        coarse[...] += mm(high, weights) + mm(low, weights)
        done = both_y[:32] + both_y[32:64]
        turn = lax.rem(k + 3, 4)
        base = (k + 3) // 4
        blocks = iota((32, SIDE), 1) // 32
        for d in range(3):
            moved = pltpu.roll(done[:, d * SIDE:(d + 1) * SIDE], turn * 32, 1)
            place = pl.ds(d * SIDE, SIDE)
            acc[base, :, place] += jnp.where(blocks >= turn, moved, 0.0)
            acc[base + 1, :, place] += jnp.where(blocks < turn, moved, 0.0)

    def land_half(k, h):
        piece = part(k, h)
        landing(piece)
        lerp_x(k * S + h * HALF, h * HALF, piece[0].size)

    more(3)
    forward(5, 0)
    land_half(7, 0)
    forward(5, 1)
    land_half(7, 1)
    compute(7)

    def step(n, carry):
        k = 6 - n

        @pl.when(k >= 4)
        def _():
            more(k - 4)

        for h in (0, 1):
            @pl.when(k >= 2)
            def _(h=h):
                forward(k - 2, h)

            land_half(k, h)
        compute(k)

        @pl.when(k == 6)
        def _():
            top_out[...] = acc[3]

            @pl.when(above)
            def _():
                up_z.start()

        return carry

    lax.fori_loop(0, CELLS - 1, step, 0)

    c_z[l] = coarse[...]
    z_turns = (2, 1, 3)
    z_copies = [
        remote(c_z.at[l], c_z.at[l], cz_s.at[o], cz_r.at[l], (g, r, lax.rem(l + o, GZ))) for o in z_turns
    ]
    for copy in z_copies:
        copy.start()

    def drain(piece):
        h2(relay, piece).wait_send()

        @pl.when(jnp.logical_not(row3))
        def _():
            s1(piece).wait_send()

        @pl.when(has_next)
        def _():
            h1(piece).wait_send()

        @pl.when(either(row0, row3))
        def _():
            s2(relay, piece).wait_send()

    def drain_cell(k, carry):
        for h in (0, 1):
            drain(part(k, h))
        return carry

    lax.fori_loop(0, CELLS - 1, drain_cell, 0)
    drain_cell(CELLS - 1, 0)

    blocks = iota((32, SIDE), 1) // 32
    packed = jnp.zeros((32, SIDE), F32)
    for d in range(3):
        packed += jnp.where(
            blocks == d, pltpu.roll(acc[0, :, pl.ds(d * SIDE, SIDE)], 32 * (d + 1), 1), 0.0
        )
    low_out[...] = packed
    down_z = remote(low_out, low_in, fine_s.at[1], fine_r.at[1], low_slab)

    @pl.when(below)
    def _():
        down_z.start()

    fold[...] = acc[pl.ds(1, 2)]

    def weigh(block, weights, at):
        high, low = split(block)
        rows = block.shape[0]
        pair = mm(jnp.concatenate([high, low], axis=0), weights[0, at, :])
        return pair[:rows] + pair[rows:] + mm(high, weights[1, at, :])

    def span(dev):
        return pl.ds(pl.multiple_of(dev * SIDE, SIDE), SIDE)

    total = weigh(coarse[...], w_z, span(l))
    for o in (1, 3, 2):
        dev = lax.rem(l + o, GZ)
        remote(c_z.at[dev], c_z.at[dev], cz_s.at[o], cz_r.at[dev], partner).wait_recv()
        total += weigh(c_z[dev], w_z, span(dev))
    slot = GY * lax.rem(g, 2) + r
    c_y[slot] = total
    y_turns = [(1, 2), (1, 1), (1, 3), (1, 0), (0, 2), (0, 1), (0, 3)]
    y_copies = [
        remote(
            c_y.at[slot], c_y.at[slot], cy_s.at[i], cy_r.at[slot],
            (mate if dx else g, lax.rem(r + o, GY), l),
        )
        for i, (dx, o) in enumerate(y_turns)
    ]
    for copy in y_copies:
        copy.start()

    @pl.when(below)
    def _():
        up_z.wait_recv()
        fold[0] += top_in[...]

    @pl.when(above)
    def _():
        down_z.wait_recv()
        for d in range(3):
            turned = pltpu.roll(low_in[...], SIDE - 32 * (d + 1), 1)
            fold[1, :, pl.ds(d * SIDE, SIDE)] += jnp.where(blocks == 3, turned, 0.0)

    up_y = remote(fold.at[:, pl.ds(24, 8)], f_y.at[0], fine_s.at[2], fine_r.at[2], high_row)
    down_y = remote(fold.at[:, pl.ds(0, 8)], f_y.at[1], fine_s.at[3], fine_r.at[3], low_row)

    @pl.when(has_high)
    def _():
        up_y.start()

    @pl.when(has_low)
    def _():
        down_y.start()

    for i, (dx, o) in reversed(list(enumerate(y_turns))):
        dev = GY * lax.rem(g + dx, 2) + lax.rem(r + o, GY)
        remote(c_y.at[dev], c_y.at[dev], cy_s.at[i], cy_r.at[dev], partner).wait_recv()
    gathered = jnp.concatenate(
        [
            jnp.concatenate(
                [c_y[GY * dx + row, pl.ds(d * 16, 16), :] for dx in range(2) for d in range(3)], axis=1
            )
            for row in range(GY)
        ],
        axis=0,
    )
    high, low = split(gathered)
    both_y = mm(m_y[...], jnp.concatenate([high, low], axis=0))
    both_y = both_y[:16] + both_y[16:]
    both_y = jnp.concatenate(
        [
            jnp.concatenate(
                [both_y[:, (dx * 3 + d) * SIDE:(dx * 3 + d + 1) * SIDE] for dx in range(2)], axis=1
            )
            for d in range(3)
        ],
        axis=0,
    )
    corr = weigh(both_y, w_x, slice(None))
    for t in range(GZ):
        c_out[t] = corr[:, t * SIDE:(t + 1) * SIDE]

    z_own = g // 2
    x_copies = [
        remote(
            c_out.at[lax.rem(z_own + o, 4)], c_x.at[z_own], cx_s.at[o], cx_r.at[z_own],
            (lax.rem(g + 2 * o, GX), r, l),
        )
        for o in (2, 1, 3)
    ]
    for copy in x_copies:
        copy.start()

    @pl.when(has_low)
    def _():
        up_y.wait_recv()
        fold[:, pl.ds(8, 8), :] += f_y[0]

    @pl.when(has_high)
    def _():
        down_y.wait_recv()
        fold[:, pl.ds(16, 8), :] += f_y[1]

    spot = lax.rem(iota((16, SIDE), 1), 32)
    parts = [
        fold[half, pl.ds(8, 16), pl.ds(d * SIDE, SIDE)] for half in range(2) for d in range(3)
    ]
    to_right, to_left = jnp.zeros((16, SIDE), F32), jnp.zeros((16, SIDE), F32)
    for n, value in enumerate(parts):
        ends = jnp.where(jnp.logical_or(spot == 24, spot == 25), value, 0.0)
        to_right += ends if n == 0 else pltpu.roll(ends, 2 * n, 1)
        ends = jnp.where(spot == 7, value, 0.0)
        to_left += ends if n == 0 else pltpu.roll(ends, n, 1)
    x_out[0] = to_right
    x_out[1] = to_left
    up_x = remote(x_out.at[0], x_in.at[0], fine_s.at[4], fine_r.at[4], right)
    down_x = remote(x_out.at[1], x_in.at[1], fine_s.at[5], fine_r.at[5], left)

    @pl.when(has_next)
    def _():
        up_x.start()

    @pl.when(has_prev)
    def _():
        down_x.start()

    @pl.when(jnp.logical_not(has_prev))
    def _():
        x_in[0] = jnp.zeros((16, SIDE), F32)

    @pl.when(jnp.logical_not(has_next))
    def _():
        x_in[1] = jnp.zeros((16, SIDE), F32)

    corr = c_out[z_own]

    def take(o):
        dev = lax.rem(z_own + o, 4)
        remote(c_x.at[dev], c_x.at[dev], cx_s.at[o], cx_r.at[dev], partner).wait_recv()
        return c_x[dev]

    @pl.when(has_prev)
    def _():
        up_x.wait_recv()

    @pl.when(has_next)
    def _():
        down_x.wait_recv()

    from_left, from_right = x_in[0], x_in[1]
    fine = []
    for n, value in enumerate(parts):
        before = pltpu.roll(from_left, SIDE - 16 - 2 * n, 1)
        after = pltpu.roll(from_right, 16 - n, 1)
        value = value + jnp.where(jnp.logical_or(spot == 8, spot == 9), before, 0.0)
        fine.append(value + jnp.where(spot == 23, after, 0.0))

    for o in (1, 3, 2):
        corr += take(o)
    for half in range(2):
        for d in range(3):
            value = fine[half * 3 + d]
            for b in range(4):
                at = (half * 4 + b) * 16
                out[d, half * 4 + b] = (
                    value[:, b * 32 + 8:b * 32 + 24] + corr[d * 16:(d + 1) * 16, at:at + 16]
                )

    @pl.when(below)
    def _():
        plane.wait_send()
        down_z.wait_send()

    @pl.when(above)
    def _():
        up_z.wait_send()

    @pl.when(has_low)
    def _():
        own_low.wait_send()
        x_low.wait_send()
        down_y.wait_send()

    @pl.when(has_high)
    def _():
        own_high.wait_send()
        x_high.wait_send()
        up_y.wait_send()

    @pl.when(has_prev)
    def _():
        t_left.wait_send()
        down_x.wait_send()

    @pl.when(has_next)
    def _():
        s_right.wait_send()
        up_x.wait_send()

    @pl.when(row2)
    def _():
        flag_up.wait_send()

    @pl.when(asks_left)
    def _():
        flag_left.wait_send()

    for copy in z_copies + y_copies + x_copies:
        copy.wait_send()


def per_device(
    fixed_image, moving_image, block_shift, fraction, brick_valid, precond_x, precond_y, precond_z
):
    dma = pltpu.SemaphoreType.DMA
    vmem = pltpu.VMEM
    brick = vmem((DEPTH + 1, SIDE, SIDE), BF16)
    hbm_spec = pl.BlockSpec(memory_space=pltpu.HBM)
    smem = pltpu.SMEM
    vmem_spec = pl.BlockSpec(memory_space=pltpu.VMEM)
    return pl.pallas_call(
        kernel,
        out_shape=jax.ShapeDtypeStruct((3, 8, 16, 16), F32),
        in_specs=[hbm_spec] * 8,
        out_specs=vmem_spec,
        scratch_shapes=[
            smem((2,), jnp.int32), smem((3,), jnp.int32), smem((1, 1, 1), jnp.int32),
            vmem((64, 64), F32), vmem((32, 32), F32), vmem((16, 16), F32),
            brick, brick, brick, brick, brick, brick,
            vmem((DEPTH, SIDE, SIDE), BF16),
            vmem((8, SIDE), F32), vmem((8, SIDE), F32),
            vmem((160, SIDE), BF16), vmem((160, SIDE), BF16), vmem((80, SIDE), BF16),
            vmem((160, SIDE), BF16), vmem((80, SIDE), BF16), vmem((80, SIDE), BF16),
            vmem((SIDE, SIDE), F32), vmem((80, SIDE), F32), vmem((80, SIDE), F32),
            vmem((S * SIDE, 256), BF16), vmem((256, 256), BF16),
            vmem((S + 1, SIDE + 8, SIDE), F32), vmem((S + 1, SIDE + 8, SIDE), F32),
            vmem((3 * SIDE, 1024), BF16), vmem((1024, 256), BF16), vmem((96, 256), BF16),
            vmem((4, 32, 384), F32), vmem((48, SIDE), F32), vmem((CELLS, SIDE, SIDE), BF16),
            vmem((2, 512, SIDE), BF16), vmem((2, 256, 512), BF16), vmem((32, SIDE), BF16),
            vmem((GZ, 48, SIDE), F32), vmem((8, 48, SIDE), F32), vmem((4, 48, SIDE), F32), vmem((4, 48, SIDE), F32),
            vmem((32, 384), F32), vmem((32, 384), F32), vmem((32, SIDE), F32), vmem((32, SIDE), F32),
            vmem((2, 2, 8, 384), F32), vmem((2, 16, SIDE), F32), vmem((2, 16, SIDE), F32),
            vmem((2, 32, 384), F32), vmem((256, 384), BF16),
            dma((8,)),
            *[dma((PIECES,))] * 8,
            dma((8,)), dma((8,)), dma((6,)), dma((6,)),
            dma((GZ,)), dma((GZ,)), dma((8,)), dma((8,)), dma((4,)), dma((4,)),
        ],
        compiler_params=pltpu.CompilerParams(
            collective_id=0, has_side_effects=True, vmem_limit_bytes=60 * 2**20
        ),
        name="registration_gradient",
    )(
        moving_image, fixed_image, block_shift.reshape(2), fraction.reshape(3),
        brick_valid, precond_x, precond_y, precond_z,
    )


def solution(mesh):
    return jax.shard_map(
        per_device,
        mesh=mesh,
        in_specs=(
            P("gz", "gy", "gx"),
            P("gz", "gy", "gx"),
            P(None, "gz", "gy", "gx"),
            P(None, "gz", "gy", "gx"),
            P("gz", "gy", "gx"),
            P(),
            P(),
            P(),
        ),
        out_specs=P(None, "gz", "gy", "gx"),
        check_vma=False,
    )
```

```python
import jax
import jax.numpy as jnp
import numpy as np
from jax import lax
from jax.experimental import pallas as pl
from jax.experimental.pallas import tpu as pltpu
from jax.sharding import PartitionSpec as P

S = 8
SIDE = 128
DEPTH = 64
CELLS = DEPTH // S
HALF = S // 2
PIECES = 2 * CELLS
GX, GY, GZ = 8, 4, 4
FULL = lax.Precision.HIGHEST
F32 = jnp.float32
BF16 = jnp.bfloat16
MESH = pl.DeviceIdType.MESH


def tap_polynomials():
    j = np.arange(S, dtype=np.float64)
    basis = np.stack(
        [np.ones(S), j + 1, (j + 1) * (j + 2) / 2, (j + 1) * (j + 2) * (j + 3) / 6], axis=1
    )
    taps = []
    for a in range(4):
        u = np.abs(j / S - (a - 1))
        taps.append(
            np.where(u < 1, 2 / 3 - u**2 + u**3 / 2, np.where(u < 2, (2 - u) ** 3 / 6, 0.0))
        )
    return np.linalg.lstsq(basis, np.stack(taps, axis=1), rcond=None)[0]


TAPS = tap_polynomials()


def iota(shape, dim):
    return lax.broadcasted_iota(jnp.int32, shape, dim)


def spline(distance):
    dist = jnp.abs(distance)
    inner = 2.0 / 3.0 - dist * dist + dist * dist * dist / 2.0
    far = 2.0 - dist
    outer = far * far * far / 6.0
    return jnp.where(dist < 1.0, inner, jnp.where(dist < 2.0, outer, 0.0))


def weight(gap):
    gap = jnp.abs(gap)
    return jnp.where(gap == 0, 0.75, jnp.where(gap == 1, 0.5, jnp.where(gap == 2, 0.125, 0.0)))


def split(value):
    high = value.astype(BF16)
    return high, (value - high.astype(F32)).astype(BF16)


def mm(a, b):
    return jnp.dot(a, b, preferred_element_type=F32)


def mm_full(a, b, dims=((1,), (0,))):
    return lax.dot_general(a, b, (dims, ((), ())), precision=FULL, preferred_element_type=F32)


def kernel(
    mov, fix, shift_h, frac_h, valid_h, px_h, py_h, pz_h, out,
    shift, frac, valid, px, py, pz,
    own, relay, land, stage, sib1, sib2, fixed,
    flag_out, flag_in, e_own, e_x, e_up, e_up_x, e_down, e_down_x, t_sel, a_bot, b_bot,
    lhs, rhs, a_buf, b_buf, mom, rhs_x, lhs_y, acc, coarse, w_c,
    w_z, w_x, m_y, c_z, c_y, c_x, c_out, top_out, top_in, low_out, low_in, f_y, x_out, x_in, fold, h_x,
    local_sem, h1_s, h1_r, h2_s, h2_r, s1_s, s1_r, s2_s, s2_r,
    edge_s, edge_r, fine_s, fine_r, cz_s, cz_r, cy_s, cy_r, cx_s, cx_r,
):
    g, r, l = lax.axis_index("gx"), lax.axis_index("gy"), lax.axis_index("gz")
    across = lax.rem(r + 2, GY)
    sibling = (g, r + 1 - 2 * lax.rem(r, 2), l)
    partner = (g, across, l)

    def remote(src, dst, send, recv, device):
        return pltpu.make_async_remote_copy(
            src_ref=src, dst_ref=dst, send_sem=send, recv_sem=recv,
            device_id=device, device_id_type=MESH,
        )

    smalls = [
        pltpu.make_async_copy(src, dst, local_sem.at[2 + i])
        for i, (src, dst) in enumerate(
            ((shift_h, shift), (frac_h, frac), (valid_h, valid), (px_h, px), (py_h, py), (pz_h, pz))
        )
    ]
    for copy in smalls:
        copy.start()
    load_own = pltpu.make_async_copy(mov, own.at[pl.ds(0, DEPTH)], local_sem.at[0])
    load_fixed = pltpu.make_async_copy(fix, fixed, local_sem.at[1])
    load_own.start()
    load_fixed.start()

    peers = [(lax.rem(g + o, GX), r, l) for o in (1, 2, 4, 6, 7)]
    peers += [(g, lax.rem(r + o, GY), l) for o in range(1, GY)]
    peers += [(g, r, lax.rem(l + o, GZ)) for o in range(1, GZ)]
    peers += [(lax.rem(g + o, GX), across, l) for o in (1, GX - 1)]
    mate = g + 1 - 2 * lax.rem(g, 2)
    peers += [(mate, lax.rem(r + o, GY), l) for o in (1, 3)]
    barrier = pltpu.get_barrier_semaphore()
    for peer in peers:
        pl.semaphore_signal(barrier, inc=1, device_id=peer, device_id_type=MESH)
    for copy in smalls:
        copy.wait()
    ox, oy = shift[0], shift[1]
    tx = frac[0].astype(F32) / 64.0
    ty = frac[1].astype(F32) / 64.0
    tz = frac[2].astype(F32) / 64.0
    live = valid[0, 0, 0].astype(F32)
    flag_out[...] = jnp.full((8, SIDE), -oy.astype(F32), F32)
    pl.semaphore_wait(barrier, len(peers))

    def part(k, h):
        if isinstance(k, int):
            return pl.ds(k * S + h * HALF, HALF + (k == CELLS - 1 and h == 1)), 2 * k + h
        return pl.ds(pl.multiple_of(k * S + h * HALF, HALF), HALF), 2 * k + h

    def source(piece):
        return own if piece[0].size > HALF else mov

    def h1(piece, src=None):
        sl, i = piece
        if src is None:
            src = source(piece)
        return remote(
            src.at[sl], relay.at[sl], h1_s.at[i], h1_r.at[i], (lax.rem(g + 1, GX), across, l)
        )

    def h2(src, piece):
        sl, i = piece
        return remote(src.at[sl], land.at[sl], h2_s.at[i], h2_r.at[i], partner)

    def s1(piece):
        sl, i = piece
        return remote(source(piece).at[sl], sib1.at[sl], s1_s.at[i], s1_r.at[i], sibling)

    def s2(src, piece):
        sl, i = piece
        return remote(src.at[sl], sib2.at[sl], s2_s.at[i], s2_r.at[i], sibling)

    has_next, has_prev = g < GX - 1, g > 0
    above, below = l < GZ - 1, l > 0
    has_low, has_high = r > 0, r < GY - 1
    row0, row1, row2, row3 = (r == i for i in range(4))
    either = jnp.logical_or

    left = (lax.rem(g + GX - 1, GX), r, l)
    right = (lax.rem(g + 1, GX), r, l)
    low_row = (g, lax.rem(r + GY - 1, GY), l)
    high_row = (g, lax.rem(r + 1, GY), l)
    low_slab = (g, r, lax.rem(l + GZ - 1, GZ))
    high_slab = (g, r, lax.rem(l + 1, GZ))

    plane = remote(mov.at[pl.ds(0, 1)], own.at[pl.ds(DEPTH, 1)], edge_s.at[6], edge_r.at[6], low_slab)
    flag_up = remote(flag_out, flag_in, edge_s.at[7], edge_r.at[7], partner)
    flag_left = remote(flag_out, flag_in, edge_s.at[7], edge_r.at[7], left)
    asks_left = jnp.logical_and(row3, has_prev)
    asked = jnp.logical_and(row3, has_next)

    def early(k):
        @pl.when(jnp.logical_and(has_next, jnp.logical_not(row3)))
        def _():
            h1(part(k, 0)).start()

    early(7)

    @pl.when(below)
    def _():
        plane.start()

    @pl.when(row2)
    def _():
        flag_up.start()

    @pl.when(asks_left)
    def _():
        flag_left.start()

    @pl.when(jnp.logical_not(row3))
    def _():
        s1(part(7, 0)).start()
        s1(part(6, 0)).start()

    early(6)

    def blend(first, second, sl):
        flagged = jnp.max(flag_in[...]) > 0.5
        for j in range(sl.size):
            z = sl.start + j
            stage[z] = jnp.where(flagged, first[z], second[z])

    def send(piece):
        @pl.when(jnp.logical_and(has_next, jnp.logical_not(row3)))
        def _():
            h1(piece).start()

        @pl.when(row3)
        def _():
            s1(piece).wait_recv()

        @pl.when(asked)
        def _():
            blend(sib1, own, piece[0])
            h1(piece, stage).start()

    zero_plane = jnp.zeros((1, SIDE, SIDE), BF16)

    @pl.when(jnp.logical_not(above))
    def _():
        own[pl.ds(DEPTH, 1)] = zero_plane

    @pl.when(jnp.logical_not(has_prev))
    def _():
        def clear(z, carry):
            relay[pl.ds(z, 1)] = zero_plane
            return carry

        lax.fori_loop(0, DEPTH + 1, clear, 0)

    load_own.wait()

    @pl.when(asked)
    def _():
        flag_left.wait_recv()

    @pl.when(row3)
    def _():
        send(part(7, 0))
        send(part(6, 0))

    lane = iota((SIDE, SIDE), 1)
    row = iota((SIDE, SIDE), 0)

    def edge_step(z, carry):
        t, s = carry
        value = own[z].astype(F32)
        t = jnp.where(lane == z, jnp.broadcast_to(value[:, 0:1], (SIDE, SIDE)), t)
        s = jnp.where(row[:80] == z, jnp.broadcast_to(value[0:1, :], (80, SIDE)), s)
        return t, s

    t_own, s_own = lax.fori_loop(
        0, DEPTH, edge_step, (jnp.zeros((SIDE, SIDE), F32), jnp.zeros((80, SIDE), F32))
    )

    @pl.when(above)
    def _():
        plane.wait_recv()

    t_own, s_own = edge_step(DEPTH, (t_own, s_own))
    rows_s, rows_t = pl.ds(0, 80), pl.ds(80, 80)
    e_own[rows_s, :] = s_own.astype(BF16)
    e_own[rows_t, :] = jnp.transpose(t_own)[:80].astype(BF16)

    s_right = remote(e_own.at[rows_s], e_x.at[rows_s], edge_s.at[0], edge_r.at[0], right)
    t_left = remote(e_own.at[rows_t], e_x.at[rows_t], edge_s.at[1], edge_r.at[1], left)
    own_low = remote(e_own, e_up, edge_s.at[2], edge_r.at[2], low_row)
    x_low = remote(e_x, e_up_x, edge_s.at[3], edge_r.at[3], low_row)
    own_high = remote(e_own.at[rows_t], e_down, edge_s.at[4], edge_r.at[4], high_row)
    x_high = remote(e_x.at[rows_t], e_down_x, edge_s.at[5], edge_r.at[5], high_row)

    @pl.when(has_next)
    def _():
        s_right.start()

    @pl.when(has_prev)
    def _():
        t_left.start()

    @pl.when(has_low)
    def _():
        own_low.start()

    @pl.when(has_high)
    def _():
        own_high.start()

    @pl.when(jnp.logical_not(row3))
    def _():
        for k, h in ((7, 1), (6, 1), (5, 0), (5, 1)):
            s1(part(k, h)).start()

    send(part(7, 1))

    moved_x, moved_y = ox != 0, oy != 0
    both = jnp.logical_and(moved_x, moved_y)

    use_own = jnp.logical_not(jnp.logical_or(moved_x, moved_y))
    only_x = jnp.logical_and(moved_x, jnp.logical_not(moved_y))
    only_y = jnp.logical_and(moved_y, jnp.logical_not(moved_x))
    use_land = either(
        only_x, either(jnp.logical_and(row2, only_y), jnp.logical_and(row3, both))
    )
    use_sib1 = jnp.logical_and(either(row1, row3), only_y)
    use_sib2 = jnp.logical_and(either(row1, row2), both)

    def choose(z):
        value = jnp.where(use_sib2, sib2[z], jnp.zeros((SIDE, SIDE), BF16))
        value = jnp.where(use_sib1, sib1[z], value)
        value = jnp.where(use_land, land[z], value)
        return jnp.where(use_own, own[z], value)

    def forward(k, h):
        piece = part(k, h)

        @pl.when(has_prev)
        def _():
            h1(piece).wait_recv()

        @pl.when(row0)
        def _():
            s1(piece).wait_recv()
            blend(sib1, relay, piece[0])
            h2(stage, piece).start()

        @pl.when(jnp.logical_not(row0))
        def _():
            h2(relay, piece).start()

        @pl.when(row3)
        def _():
            s2(relay, piece).start()

        if isinstance(k, int) and k >= 6:
            send(part(*{(7, 0): (6, 1), (6, 0): (5, 0), (7, 1): (5, 1), (6, 1): (4, 0)}[k, h]))
        else:
            @pl.when(k >= 1 + h)
            def _():
                send(part(k - 1 - h, 1 - h))

    def landing(piece):
        h2(relay, piece).wait_recv()

        @pl.when(row0)
        def _():
            s2(land, piece).start()

        @pl.when(row1)
        def _():
            s1(piece).wait_recv()

        @pl.when(either(row1, row2))
        def _():
            s2(relay, piece).wait_recv()

    up_z = remote(top_out, top_in, fine_s.at[0], fine_r.at[0], high_slab)

    @pl.when(row0)
    def _():
        flag_up.wait_recv()

    forward(7, 0)

    rhs_lane = iota((2 * SIDE, 2 * SIDE), 1)
    rhs_row = iota((2 * SIDE, 2 * SIDE), 0)
    col = lax.rem(rhs_lane, SIDE)
    is_lerp = rhs_lane < SIDE
    here = jnp.where(is_lerp, 1.0 - tx, -1.0)
    there = jnp.where(is_lerp, tx, 1.0)
    top = jnp.where(rhs_row == col, here, jnp.where(rhs_row == col + 1, there, 0.0))
    rhs[...] = jnp.where(
        rhs_row < SIDE, top, jnp.where(col == SIDE - 1, there, 0.0)
    ).astype(BF16)

    point = lax.rem(lane, 32) - 8
    tap = lane // 32
    px_ok = jnp.logical_and(g * 16 + point >= 0, g * 16 + point < 16 * GX)
    basis_x = jnp.where(px_ok, spline(row.astype(F32) / S - point.astype(F32)), 0.0)
    for m in range(4):
        scale = jnp.full((SIDE, SIDE), float(TAPS[m, 3]), F32)
        for a in (2, 1, 0):
            scale = jnp.where(tap == a, float(TAPS[m, a]), scale)
        high, low = split(basis_x * scale)
        for half in range(2):
            rhs_x[pl.ds(m * 256 + half * 128, 128), pl.ds(0, 128)] = high
            rhs_x[pl.ds(m * 256 + half * 128, 128), pl.ds(128, 128)] = low

    q_point = iota((32, SIDE), 0) - 8
    q_ok = jnp.logical_and(r * 16 + q_point >= 0, r * 16 + q_point < 16 * GY)
    basis_y = jnp.where(
        q_ok, spline(iota((32, SIDE), 1).astype(F32) / S - q_point.astype(F32)), 0.0
    ) * (live * S ** (-1.5))
    high, low = split(basis_y)
    lhs_y[pl.ds(0, 32), pl.ds(0, 128)] = high
    lhs_y[pl.ds(0, 32), pl.ds(128, 128)] = high
    lhs_y[pl.ds(32, 32), pl.ds(0, 128)] = low
    lhs_y[pl.ds(32, 32), pl.ds(128, 128)] = jnp.zeros((32, SIDE), BF16)

    coarse_y = mm_full(weight(iota((16, 32), 1) - 8 - 2 * (iota((16, 32), 0) - 1)), basis_y)
    high, low = split(coarse_y)
    lhs_y[pl.ds(64, 16), pl.ds(0, 128)] = high
    lhs_y[pl.ds(64, 16), pl.ds(128, 128)] = high
    lhs_y[pl.ds(80, 16), pl.ds(0, 128)] = low
    lhs_y[pl.ds(80, 16), pl.ds(128, 128)] = jnp.zeros((16, SIDE), BF16)

    def cell_weights(k, carry):
        z_point = k + row // 32 - 1
        z_ok = jnp.logical_and(l * 8 + z_point >= 0, l * 8 + z_point < 8 * GZ)
        both_w = weight(z_point - 2 * (lane // 16 - 1)) * weight(
            lax.rem(row, 32) - 8 - 2 * (lax.rem(lane, 16) - 1)
        )
        w_c[k] = jnp.where(z_ok, both_w, 0.0).astype(BF16)
        return carry

    lax.fori_loop(0, CELLS, cell_weights, 0)
    coarse[...] = jnp.zeros((48, SIDE), F32)
    wr, wl = iota((512, SIDE), 0), iota((512, SIDE), 1)

    forward(6, 0)

    def arrive(copy, dst, ok):
        @pl.when(ok)
        def _():
            copy.wait_recv()

        @pl.when(jnp.logical_not(ok))
        def _():
            dst[...] = jnp.zeros(dst.shape, BF16)

    arrive(s_right, e_x.at[rows_s], has_prev)
    arrive(t_left, e_x.at[rows_t], has_next)

    @pl.when(has_low)
    def _():
        x_low.start()

    @pl.when(has_high)
    def _():
        x_high.start()

    kz = 4 * (iota((512, 16), 0) // 128) + lax.rem(iota((512, 16), 0) // 16, 8) - 1
    pick_z = (kz == iota((512, 16), 1)).astype(F32)
    spread_z = weight(l * 8 + iota((16, SIDE), 1) // 16 - 2 * iota((16, SIDE), 0))
    full_z = mm_full(mm_full(pick_z, pz[...], ((1,), (1,))), spread_z)
    full_z = jnp.where(lax.rem(wr, 16) == lax.rem(wl, 16), full_z, 0.0)
    high, low = split(full_z)
    w_z[0], w_z[1] = high, low

    jy = 8 * (iota((32, 64), 1) // 16) + lax.rem(iota((32, 64), 1), 16) - 1
    pick_y = (jy == iota((32, 64), 0)).astype(F32)
    spread_y = weight(r * 16 + iota((16, 32), 0) - 2 * iota((16, 32), 1))
    full_y = mm_full(spread_y, mm_full(py[...], pick_y))
    high, low = split(full_y)
    m_y[...] = jnp.concatenate(
        [
            jnp.concatenate([high.astype(F32), high.astype(F32)], axis=1),
            jnp.concatenate([low.astype(F32), jnp.zeros((16, 64), F32)], axis=1),
        ],
        axis=0,
    ).astype(BF16)

    xl = iota((64, 512), 1)
    spread_x = weight(16 * (2 * (xl // 128) + lax.rem(g, 2)) + lax.rem(xl, 16) - 2 * iota((64, 512), 0))
    kx = 8 * (g - lax.rem(g, 2) + iota((256, 64), 0) // 128) + lax.rem(iota((256, 64), 0), 16) - 1
    pick_x = (kx == iota((256, 64), 1)).astype(F32)
    full_x = mm_full(pick_x, mm_full(px[...], spread_x, ((0,), (0,))))
    same = lax.rem(iota((256, 512), 0) // 16, 8) == lax.rem(iota((256, 512), 1) // 16, 8)
    high, low = split(jnp.where(same, full_x, 0.0))
    w_x[0], w_x[1] = high, low

    def clear_acc(i, carry):
        acc[i] = jnp.zeros((32, 384), F32)
        return carry

    lax.fori_loop(0, 4, clear_acc, 0)

    arrive(own_low, e_up, has_high)
    arrive(own_high, e_down, has_low)
    arrive(x_low, e_up_x, has_high)
    arrive(x_high, e_down_x, has_low)

    def pick(stay, by_x, by_y, by_both):
        return jnp.where(moved_y, jnp.where(moved_x, by_both, by_y), jnp.where(moved_x, by_x, stay))

    def wide(ref, rows):
        return ref[rows, :].astype(F32)

    t_here, t_right = wide(e_own, rows_t), wide(e_x, rows_t)
    t_wide = pick(t_right, t_here, e_down_x[...].astype(F32), e_down[...].astype(F32))
    t_sel[...] = jnp.transpose(jnp.concatenate([t_wide, jnp.zeros((48, SIDE), F32)], axis=0))
    s_sel = pick(wide(e_up, rows_s), wide(e_up_x, rows_s), wide(e_own, rows_s), wide(e_x, rows_s))
    k_sel = pick(wide(e_up_x, rows_t), wide(e_up, rows_t), t_right, t_here)
    diag = jnp.where(lane[:80] == row[:80], jnp.broadcast_to(k_sel[:, 0:1], (80, SIDE)), 0.0)
    bottom = mm(jnp.concatenate([s_sel, diag], axis=1).astype(BF16), rhs[...])
    a_bot[...] = bottom[:, :SIDE]
    b_bot[...] = bottom[:, SIDE:]

    load_fixed.wait()

    def fill(z, j):
        lhs[pl.ds(j * SIDE, SIDE), pl.ds(0, SIDE)] = choose(z)
        lhs[pl.ds(j * SIDE, SIDE), pl.ds(SIDE, SIDE)] = jnp.where(lane == z, t_sel[...], 0.0).astype(BF16)

    def lerp_x(z, slot, count):
        for j in range(count):
            fill(z + j, j)
        both_x = mm(lhs[pl.ds(0, count * SIDE), :], rhs[...])
        for j in range(count):
            rows = slice(j * SIDE, (j + 1) * SIDE)
            a_buf[slot + j, pl.ds(0, SIDE), :] = both_x[rows, :SIDE]
            b_buf[slot + j, pl.ds(0, SIDE), :] = both_x[rows, SIDE:]
            a_buf[slot + j, pl.ds(SIDE, 1), :] = a_bot[pl.ds(z + j, 1), :]
            b_buf[slot + j, pl.ds(SIDE, 1), :] = b_bot[pl.ds(z + j, 1), :]

    def rows_of(j, y0):
        a = a_buf[j, pl.ds(y0, 16), :]
        b = b_buf[j, pl.ds(y0, 16), :]
        dy = a_buf[j, pl.ds(y0 + 1, 16), :] - a
        along_xy = a + ty * dy
        diff_xy = b + ty * (b_buf[j, pl.ds(y0 + 1, 16), :] - b)
        return along_xy, diff_xy, dy

    def compute(k):
        def tile(t, carry):
            y0 = pl.multiple_of(t * 16, 16)
            w1, x1, y1 = rows_of(S, y0)
            sums = [[jnp.zeros((16, SIDE), F32) for _ in range(4)] for _ in range(3)]
            for j in reversed(range(S)):
                w0, x0, yy0 = rows_of(j, y0)
                gz = w1 - w0
                res = w0 + tz * gz - fixed[k * S + j, pl.ds(y0, 16), :].astype(F32)
                grads = (x0 + tz * (x1 - x0), yy0 + tz * (y1 - yy0), gz)
                for d in range(3):
                    value = res * grads[d]
                    for m in range(4):
                        value = sums[d][m] + value
                        sums[d][m] = value
                w1, x1, y1 = w0, x0, yy0
            for d in range(3):
                for m in range(4):
                    high, low = split(sums[d][m])
                    place = pl.ds(pl.multiple_of(d * SIDE + y0, 16), 16)
                    mom[place, pl.ds(m * 256, 128)] = high
                    mom[place, pl.ds(m * 256 + 128, 128)] = low
            return carry

        lax.fori_loop(0, SIDE // 16, tile, 0)
        a_buf[S] = a_buf[0]
        b_buf[S] = b_buf[0]

        parts = mm(mom[...], rhs_x[...])
        parts = parts[:, :SIDE] + parts[:, SIDE:]
        wide = jnp.concatenate([parts[d * SIDE:(d + 1) * SIDE] for d in range(3)], axis=1)
        high, low = split(wide)
        h_x[pl.ds(0, SIDE), :] = high
        h_x[pl.ds(SIDE, SIDE), :] = low
        both_y = mm(lhs_y[...], h_x[...])
        rough = both_y[64:80] + both_y[80:96]
        rough = jnp.concatenate([rough[:, d * SIDE:(d + 1) * SIDE] for d in range(3)], axis=0)
        high, low = split(rough)
        weights = w_c[k]
        coarse[...] += mm(high, weights) + mm(low, weights)
        done = both_y[:32] + both_y[32:64]
        turn = lax.rem(k + 3, 4)
        base = (k + 3) // 4
        blocks = iota((32, SIDE), 1) // 32
        for d in range(3):
            moved = pltpu.roll(done[:, d * SIDE:(d + 1) * SIDE], turn * 32, 1)
            place = pl.ds(d * SIDE, SIDE)
            acc[base, :, place] += jnp.where(blocks >= turn, moved, 0.0)
            acc[base + 1, :, place] += jnp.where(blocks < turn, moved, 0.0)

    def land_half(k, h):
        piece = part(k, h)
        landing(piece)
        lerp_x(k * S + h * HALF, h * HALF, piece[0].size)

    def more(k):
        @pl.when(jnp.logical_not(row3))
        def _():
            for h in (0, 1):
                s1(part(k, h)).start()

    more(4)
    forward(7, 1)
    land_half(7, 0)
    forward(6, 1)
    land_half(7, 1)
    compute(7)

    def step(n, carry):
        k = 6 - n

        @pl.when(k >= 3)
        def _():
            more(k - 3)

        for h in (0, 1):
            @pl.when(k >= 1)
            def _(h=h):
                forward(k - 1, h)

            land_half(k, h)
        compute(k)

        @pl.when(k == 6)
        def _():
            top_out[...] = acc[3]

            @pl.when(above)
            def _():
                up_z.start()

        return carry

    lax.fori_loop(0, CELLS - 1, step, 0)

    c_z[l] = coarse[...]
    z_turns = (2, 1, 3)
    z_copies = [
        remote(c_z.at[l], c_z.at[l], cz_s.at[o], cz_r.at[l], (g, r, lax.rem(l + o, GZ))) for o in z_turns
    ]
    for copy in z_copies:
        copy.start()

    def drain(piece):
        h2(relay, piece).wait_send()

        @pl.when(jnp.logical_not(row3))
        def _():
            s1(piece).wait_send()

        @pl.when(has_next)
        def _():
            h1(piece).wait_send()

        @pl.when(either(row0, row3))
        def _():
            s2(relay, piece).wait_send()

    def drain_cell(k, carry):
        for h in (0, 1):
            drain(part(k, h))
        return carry

    lax.fori_loop(0, CELLS - 1, drain_cell, 0)
    drain_cell(CELLS - 1, 0)

    blocks = iota((32, SIDE), 1) // 32
    packed = jnp.zeros((32, SIDE), F32)
    for d in range(3):
        packed += jnp.where(
            blocks == d, pltpu.roll(acc[0, :, pl.ds(d * SIDE, SIDE)], 32 * (d + 1), 1), 0.0
        )
    low_out[...] = packed
    down_z = remote(low_out, low_in, fine_s.at[1], fine_r.at[1], low_slab)

    @pl.when(below)
    def _():
        down_z.start()

    fold[...] = acc[pl.ds(1, 2)]

    def weigh(block, weights, at):
        high, low = split(block)
        rows = block.shape[0]
        pair = mm(jnp.concatenate([high, low], axis=0), weights[0, at, :])
        return pair[:rows] + pair[rows:] + mm(high, weights[1, at, :])

    def span(dev):
        return pl.ds(pl.multiple_of(dev * SIDE, SIDE), SIDE)

    total = weigh(coarse[...], w_z, span(l))
    for o in (1, 3, 2):
        dev = lax.rem(l + o, GZ)
        remote(c_z.at[dev], c_z.at[dev], cz_s.at[o], cz_r.at[dev], partner).wait_recv()
        total += weigh(c_z[dev], w_z, span(dev))
    slot = GY * lax.rem(g, 2) + r
    c_y[slot] = total
    y_turns = [(1, 2), (1, 1), (1, 3), (1, 0), (0, 2), (0, 1), (0, 3)]
    y_copies = [
        remote(
            c_y.at[slot], c_y.at[slot], cy_s.at[i], cy_r.at[slot],
            (mate if dx else g, lax.rem(r + o, GY), l),
        )
        for i, (dx, o) in enumerate(y_turns)
    ]
    for copy in y_copies:
        copy.start()

    @pl.when(below)
    def _():
        up_z.wait_recv()
        fold[0] += top_in[...]

    @pl.when(above)
    def _():
        down_z.wait_recv()
        for d in range(3):
            turned = pltpu.roll(low_in[...], SIDE - 32 * (d + 1), 1)
            fold[1, :, pl.ds(d * SIDE, SIDE)] += jnp.where(blocks == 3, turned, 0.0)

    up_y = remote(fold.at[:, pl.ds(24, 8)], f_y.at[0], fine_s.at[2], fine_r.at[2], high_row)
    down_y = remote(fold.at[:, pl.ds(0, 8)], f_y.at[1], fine_s.at[3], fine_r.at[3], low_row)

    @pl.when(has_high)
    def _():
        up_y.start()

    @pl.when(has_low)
    def _():
        down_y.start()

    for i, (dx, o) in reversed(list(enumerate(y_turns))):
        dev = GY * lax.rem(g + dx, 2) + lax.rem(r + o, GY)
        remote(c_y.at[dev], c_y.at[dev], cy_s.at[i], cy_r.at[dev], partner).wait_recv()
    gathered = jnp.concatenate(
        [
            jnp.concatenate(
                [c_y[GY * dx + row, pl.ds(d * 16, 16), :] for dx in range(2) for d in range(3)], axis=1
            )
            for row in range(GY)
        ],
        axis=0,
    )
    high, low = split(gathered)
    both_y = mm(m_y[...], jnp.concatenate([high, low], axis=0))
    both_y = both_y[:16] + both_y[16:]
    both_y = jnp.concatenate(
        [
            jnp.concatenate(
                [both_y[:, (dx * 3 + d) * SIDE:(dx * 3 + d + 1) * SIDE] for dx in range(2)], axis=1
            )
            for d in range(3)
        ],
        axis=0,
    )
    corr = weigh(both_y, w_x, slice(None))
    for t in range(GZ):
        c_out[t] = corr[:, t * SIDE:(t + 1) * SIDE]

    z_own = g // 2
    x_copies = [
        remote(
            c_out.at[lax.rem(z_own + o, 4)], c_x.at[z_own], cx_s.at[o], cx_r.at[z_own],
            (lax.rem(g + 2 * o, GX), r, l),
        )
        for o in (2, 1, 3)
    ]
    for copy in x_copies:
        copy.start()

    @pl.when(has_low)
    def _():
        up_y.wait_recv()
        fold[:, pl.ds(8, 8), :] += f_y[0]

    @pl.when(has_high)
    def _():
        down_y.wait_recv()
        fold[:, pl.ds(16, 8), :] += f_y[1]

    spot = lax.rem(iota((16, SIDE), 1), 32)
    parts = [
        fold[half, pl.ds(8, 16), pl.ds(d * SIDE, SIDE)] for half in range(2) for d in range(3)
    ]
    to_right, to_left = jnp.zeros((16, SIDE), F32), jnp.zeros((16, SIDE), F32)
    for n, value in enumerate(parts):
        ends = jnp.where(jnp.logical_or(spot == 24, spot == 25), value, 0.0)
        to_right += ends if n == 0 else pltpu.roll(ends, 2 * n, 1)
        ends = jnp.where(spot == 7, value, 0.0)
        to_left += ends if n == 0 else pltpu.roll(ends, n, 1)
    x_out[0] = to_right
    x_out[1] = to_left
    up_x = remote(x_out.at[0], x_in.at[0], fine_s.at[4], fine_r.at[4], right)
    down_x = remote(x_out.at[1], x_in.at[1], fine_s.at[5], fine_r.at[5], left)

    @pl.when(has_next)
    def _():
        up_x.start()

    @pl.when(has_prev)
    def _():
        down_x.start()

    @pl.when(jnp.logical_not(has_prev))
    def _():
        x_in[0] = jnp.zeros((16, SIDE), F32)

    @pl.when(jnp.logical_not(has_next))
    def _():
        x_in[1] = jnp.zeros((16, SIDE), F32)

    corr = c_out[z_own]

    def take(o):
        dev = lax.rem(z_own + o, 4)
        remote(c_x.at[dev], c_x.at[dev], cx_s.at[o], cx_r.at[dev], partner).wait_recv()
        return c_x[dev]

    @pl.when(has_prev)
    def _():
        up_x.wait_recv()

    @pl.when(has_next)
    def _():
        down_x.wait_recv()

    from_left, from_right = x_in[0], x_in[1]
    fine = []
    for n, value in enumerate(parts):
        before = pltpu.roll(from_left, SIDE - 16 - 2 * n, 1)
        after = pltpu.roll(from_right, 16 - n, 1)
        value = value + jnp.where(jnp.logical_or(spot == 8, spot == 9), before, 0.0)
        fine.append(value + jnp.where(spot == 23, after, 0.0))

    for o in (1, 3, 2):
        corr += take(o)
    for half in range(2):
        for d in range(3):
            value = fine[half * 3 + d]
            for b in range(4):
                at = (half * 4 + b) * 16
                out[d, half * 4 + b] = (
                    value[:, b * 32 + 8:b * 32 + 24] + corr[d * 16:(d + 1) * 16, at:at + 16]
                )

    @pl.when(below)
    def _():
        plane.wait_send()
        down_z.wait_send()

    @pl.when(above)
    def _():
        up_z.wait_send()

    @pl.when(has_low)
    def _():
        own_low.wait_send()
        x_low.wait_send()
        down_y.wait_send()

    @pl.when(has_high)
    def _():
        own_high.wait_send()
        x_high.wait_send()
        up_y.wait_send()

    @pl.when(has_prev)
    def _():
        t_left.wait_send()
        down_x.wait_send()

    @pl.when(has_next)
    def _():
        s_right.wait_send()
        up_x.wait_send()

    @pl.when(row2)
    def _():
        flag_up.wait_send()

    @pl.when(asks_left)
    def _():
        flag_left.wait_send()

    for copy in z_copies + y_copies + x_copies:
        copy.wait_send()


def per_device(
    fixed_image, moving_image, block_shift, fraction, brick_valid, precond_x, precond_y, precond_z
):
    dma = pltpu.SemaphoreType.DMA
    vmem = pltpu.VMEM
    brick = vmem((DEPTH + 1, SIDE, SIDE), BF16)
    hbm_spec = pl.BlockSpec(memory_space=pltpu.HBM)
    smem = pltpu.SMEM
    vmem_spec = pl.BlockSpec(memory_space=pltpu.VMEM)
    return pl.pallas_call(
        kernel,
        out_shape=jax.ShapeDtypeStruct((3, 8, 16, 16), F32),
        in_specs=[hbm_spec] * 8,
        out_specs=vmem_spec,
        scratch_shapes=[
            smem((2,), jnp.int32), smem((3,), jnp.int32), smem((1, 1, 1), jnp.int32),
            vmem((64, 64), F32), vmem((32, 32), F32), vmem((16, 16), F32),
            brick, brick, brick, brick, brick, brick,
            vmem((DEPTH, SIDE, SIDE), BF16),
            vmem((8, SIDE), F32), vmem((8, SIDE), F32),
            vmem((160, SIDE), BF16), vmem((160, SIDE), BF16), vmem((160, SIDE), BF16),
            vmem((160, SIDE), BF16), vmem((80, SIDE), BF16), vmem((80, SIDE), BF16),
            vmem((SIDE, SIDE), F32), vmem((80, SIDE), F32), vmem((80, SIDE), F32),
            vmem((S * SIDE, 256), BF16), vmem((256, 256), BF16),
            vmem((S + 1, SIDE + 8, SIDE), F32), vmem((S + 1, SIDE + 8, SIDE), F32),
            vmem((3 * SIDE, 1024), BF16), vmem((1024, 256), BF16), vmem((96, 256), BF16),
            vmem((4, 32, 384), F32), vmem((48, SIDE), F32), vmem((CELLS, SIDE, SIDE), BF16),
            vmem((2, 512, SIDE), BF16), vmem((2, 256, 512), BF16), vmem((32, SIDE), BF16),
            vmem((GZ, 48, SIDE), F32), vmem((8, 48, SIDE), F32), vmem((4, 48, SIDE), F32), vmem((4, 48, SIDE), F32),
            vmem((32, 384), F32), vmem((32, 384), F32), vmem((32, SIDE), F32), vmem((32, SIDE), F32),
            vmem((2, 2, 8, 384), F32), vmem((2, 16, SIDE), F32), vmem((2, 16, SIDE), F32),
            vmem((2, 32, 384), F32), vmem((256, 384), BF16),
            dma((8,)),
            *[dma((PIECES,))] * 8,
            dma((8,)), dma((8,)), dma((6,)), dma((6,)),
            dma((GZ,)), dma((GZ,)), dma((8,)), dma((8,)), dma((4,)), dma((4,)),
        ],
        compiler_params=pltpu.CompilerParams(
            collective_id=0, has_side_effects=True, vmem_limit_bytes=53 * 2**20
        ),
        name="registration_gradient",
    )(
        *(
            pltpu.with_memory_space_constraint(x, pltpu.HBM)
            for x in (
                moving_image, fixed_image, block_shift.reshape(2), fraction.reshape(3)
            )
        ),
        brick_valid,
        *(pltpu.with_memory_space_constraint(x, pltpu.HBM) for x in (precond_x, precond_y, precond_z)),
    )


def solution(mesh):
    return jax.shard_map(
        per_device,
        mesh=mesh,
        in_specs=(
            P("gz", "gy", "gx"),
            P("gz", "gy", "gx"),
            P(None, "gz", "gy", "gx"),
            P(None, "gz", "gy", "gx"),
            P("gz", "gy", "gx"),
            P(),
            P(),
            P(),
        ),
        out_specs=P(None, "gz", "gy", "gx"),
        check_vma=False,
    )
```

```python
import jax
import jax.numpy as jnp
import numpy as np
from jax import lax
from jax.experimental import pallas as pl
from jax.experimental.pallas import tpu as pltpu
from jax.sharding import PartitionSpec as P

S = 8
SIDE = 128
DEPTH = 64
CELLS = DEPTH // S
HALF = S // 2
PIECES = 2 * CELLS
GX, GY, GZ = 8, 4, 4
FULL = lax.Precision.HIGHEST
F32 = jnp.float32
BF16 = jnp.bfloat16
MESH = pl.DeviceIdType.MESH


def tap_polynomials():
    j = np.arange(S, dtype=np.float64)
    basis = np.stack(
        [np.ones(S), j + 1, (j + 1) * (j + 2) / 2, (j + 1) * (j + 2) * (j + 3) / 6], axis=1
    )
    taps = []
    for a in range(4):
        u = np.abs(j / S - (a - 1))
        taps.append(
            np.where(u < 1, 2 / 3 - u**2 + u**3 / 2, np.where(u < 2, (2 - u) ** 3 / 6, 0.0))
        )
    return np.linalg.lstsq(basis, np.stack(taps, axis=1), rcond=None)[0]


TAPS = tap_polynomials()


def iota(shape, dim):
    return lax.broadcasted_iota(jnp.int32, shape, dim)


def spline(distance):
    dist = jnp.abs(distance)
    inner = 2.0 / 3.0 - dist * dist + dist * dist * dist / 2.0
    far = 2.0 - dist
    outer = far * far * far / 6.0
    return jnp.where(dist < 1.0, inner, jnp.where(dist < 2.0, outer, 0.0))


def weight(gap):
    gap = jnp.abs(gap)
    return jnp.where(gap == 0, 0.75, jnp.where(gap == 1, 0.5, jnp.where(gap == 2, 0.125, 0.0)))


def split(value):
    high = value.astype(BF16)
    return high, (value - high.astype(F32)).astype(BF16)


def mm(a, b):
    return jnp.dot(a, b, preferred_element_type=F32)


def mm_full(a, b, dims=((1,), (0,))):
    return lax.dot_general(a, b, (dims, ((), ())), precision=FULL, preferred_element_type=F32)


def kernel(
    mov, fix, shift_h, frac_h, valid_h, px_h, py_h, pz_h, out,
    shift, frac, valid, px, py, pz,
    own, relay, land, stage, sib1, sib2, fixed,
    flag_out, flag_in, e_own, e_x, e_up, e_up_x, e_down, e_down_x, t_sel, a_bot, b_bot,
    lhs, rhs, a_buf, b_buf, mom, rhs_x, lhs_y, acc, coarse, w_c,
    w_z, w_x, m_y, c_z, c_y, c_x, c_out, top_out, top_in, low_out, low_in, f_y, x_out, x_in, fold, h_x,
    local_sem, h1_s, h1_r, h2_s, h2_r, s1_s, s1_r, s2_s, s2_r,
    edge_s, edge_r, fine_s, fine_r, cz_s, cz_r, cy_s, cy_r, cx_s, cx_r,
):
    g, r, l = lax.axis_index("gx"), lax.axis_index("gy"), lax.axis_index("gz")
    across = lax.rem(r + 2, GY)
    sibling = (g, r + 1 - 2 * lax.rem(r, 2), l)
    partner = (g, across, l)

    def remote(src, dst, send, recv, device):
        return pltpu.make_async_remote_copy(
            src_ref=src, dst_ref=dst, send_sem=send, recv_sem=recv,
            device_id=device, device_id_type=MESH,
        )

    peers = [(lax.rem(g + o, GX), r, l) for o in (1, 2, 4, 6, 7)]
    peers += [(g, lax.rem(r + o, GY), l) for o in range(1, GY)]
    peers += [(g, r, lax.rem(l + o, GZ)) for o in range(1, GZ)]
    peers += [(lax.rem(g + o, GX), across, l) for o in (1, GX - 1)]
    mate = g + 1 - 2 * lax.rem(g, 2)
    peers += [(mate, lax.rem(r + o, GY), l) for o in (1, 3)]
    barrier = pltpu.get_barrier_semaphore()
    for peer in peers:
        pl.semaphore_signal(barrier, inc=1, device_id=peer, device_id_type=MESH)
    smalls = [
        pltpu.make_async_copy(src, dst, local_sem.at[2 + i])
        for i, (src, dst) in enumerate(
            ((shift_h, shift), (frac_h, frac), (valid_h, valid), (px_h, px), (py_h, py), (pz_h, pz))
        )
    ]
    for copy in smalls:
        copy.start()
    load_own = pltpu.make_async_copy(mov, own.at[pl.ds(0, DEPTH)], local_sem.at[0])
    load_fixed = pltpu.make_async_copy(fix, fixed, local_sem.at[1])
    load_own.start()
    load_fixed.start()

    for copy in smalls:
        copy.wait()
    ox, oy = shift[0], shift[1]
    tx = frac[0].astype(F32) / 64.0
    ty = frac[1].astype(F32) / 64.0
    tz = frac[2].astype(F32) / 64.0
    live = valid[0, 0, 0].astype(F32)
    flag_out[...] = jnp.full((8, SIDE), -oy.astype(F32), F32)
    pl.semaphore_wait(barrier, len(peers))

    def part(k, h):
        if isinstance(k, int):
            return pl.ds(k * S + h * HALF, HALF + (k == CELLS - 1 and h == 1)), 2 * k + h
        return pl.ds(pl.multiple_of(k * S + h * HALF, HALF), HALF), 2 * k + h

    def source(piece):
        return own if piece[0].size > HALF else mov

    def h1(piece, src=None):
        sl, i = piece
        if src is None:
            src = source(piece)
        return remote(
            src.at[sl], relay.at[sl], h1_s.at[i], h1_r.at[i], (lax.rem(g + 1, GX), across, l)
        )

    def h2(src, piece):
        sl, i = piece
        return remote(src.at[sl], land.at[sl], h2_s.at[i], h2_r.at[i], partner)

    def s1(piece):
        sl, i = piece
        return remote(source(piece).at[sl], sib1.at[sl], s1_s.at[i], s1_r.at[i], sibling)

    def s2(src, piece):
        sl, i = piece
        return remote(src.at[sl], sib2.at[sl], s2_s.at[i], s2_r.at[i], sibling)

    has_next, has_prev = g < GX - 1, g > 0
    above, below = l < GZ - 1, l > 0
    has_low, has_high = r > 0, r < GY - 1
    row0, row1, row2, row3 = (r == i for i in range(4))
    either = jnp.logical_or

    left = (lax.rem(g + GX - 1, GX), r, l)
    right = (lax.rem(g + 1, GX), r, l)
    low_row = (g, lax.rem(r + GY - 1, GY), l)
    high_row = (g, lax.rem(r + 1, GY), l)
    low_slab = (g, r, lax.rem(l + GZ - 1, GZ))
    high_slab = (g, r, lax.rem(l + 1, GZ))

    plane = remote(mov.at[pl.ds(0, 1)], own.at[pl.ds(DEPTH, 1)], edge_s.at[6], edge_r.at[6], low_slab)
    flag_up = remote(flag_out, flag_in, edge_s.at[7], edge_r.at[7], partner)
    flag_left = remote(flag_out, flag_in, edge_s.at[7], edge_r.at[7], left)
    asks_left = jnp.logical_and(row3, has_prev)
    asked = jnp.logical_and(row3, has_next)

    def early(k):
        @pl.when(jnp.logical_and(has_next, jnp.logical_not(row3)))
        def _():
            h1(part(k, 0)).start()

    early(7)

    @pl.when(below)
    def _():
        plane.start()

    @pl.when(row2)
    def _():
        flag_up.start()

    @pl.when(asks_left)
    def _():
        flag_left.start()

    @pl.when(jnp.logical_not(row3))
    def _():
        s1(part(7, 0)).start()
        s1(part(6, 0)).start()

    early(6)

    def blend(first, second, sl):
        flagged = jnp.max(flag_in[...]) > 0.5
        for j in range(sl.size):
            z = sl.start + j
            stage[z] = jnp.where(flagged, first[z], second[z])

    def send(piece):
        @pl.when(jnp.logical_and(has_next, jnp.logical_not(row3)))
        def _():
            h1(piece).start()

        @pl.when(row3)
        def _():
            s1(piece).wait_recv()

        @pl.when(asked)
        def _():
            blend(sib1, own, piece[0])
            h1(piece, stage).start()

    zero_plane = jnp.zeros((1, SIDE, SIDE), BF16)

    @pl.when(jnp.logical_not(above))
    def _():
        own[pl.ds(DEPTH, 1)] = zero_plane

    @pl.when(jnp.logical_not(has_prev))
    def _():
        def clear(z, carry):
            relay[pl.ds(z, 1)] = zero_plane
            return carry

        lax.fori_loop(0, DEPTH + 1, clear, 0)

    load_own.wait()

    @pl.when(asked)
    def _():
        flag_left.wait_recv()

    @pl.when(row3)
    def _():
        send(part(7, 0))
        send(part(6, 0))

    lane = iota((SIDE, SIDE), 1)
    row = iota((SIDE, SIDE), 0)

    def edge_step(z, carry):
        t, s = carry
        value = own[z].astype(F32)
        t = jnp.where(lane == z, jnp.broadcast_to(value[:, 0:1], (SIDE, SIDE)), t)
        s = jnp.where(row[:80] == z, jnp.broadcast_to(value[0:1, :], (80, SIDE)), s)
        return t, s

    t_own, s_own = lax.fori_loop(
        0, DEPTH, edge_step, (jnp.zeros((SIDE, SIDE), F32), jnp.zeros((80, SIDE), F32))
    )

    @pl.when(above)
    def _():
        plane.wait_recv()

    t_own, s_own = edge_step(DEPTH, (t_own, s_own))
    rows_s, rows_t = pl.ds(0, 80), pl.ds(80, 80)
    e_own[rows_s, :] = s_own.astype(BF16)
    e_own[rows_t, :] = jnp.transpose(t_own)[:80].astype(BF16)

    s_right = remote(e_own.at[rows_s], e_x.at[rows_s], edge_s.at[0], edge_r.at[0], right)
    t_left = remote(e_own.at[rows_t], e_x.at[rows_t], edge_s.at[1], edge_r.at[1], left)
    own_low = remote(e_own, e_up, edge_s.at[2], edge_r.at[2], low_row)
    x_low = remote(e_x, e_up_x, edge_s.at[3], edge_r.at[3], low_row)
    own_high = remote(e_own.at[rows_t], e_down, edge_s.at[4], edge_r.at[4], high_row)
    x_high = remote(e_x.at[rows_t], e_down_x, edge_s.at[5], edge_r.at[5], high_row)

    @pl.when(has_next)
    def _():
        s_right.start()

    @pl.when(has_prev)
    def _():
        t_left.start()

    @pl.when(has_low)
    def _():
        own_low.start()

    @pl.when(has_high)
    def _():
        own_high.start()

    @pl.when(jnp.logical_not(row3))
    def _():
        for k, h in ((7, 1), (6, 1), (5, 0), (5, 1)):
            s1(part(k, h)).start()

    send(part(7, 1))

    moved_x, moved_y = ox != 0, oy != 0
    both = jnp.logical_and(moved_x, moved_y)

    use_own = jnp.logical_not(jnp.logical_or(moved_x, moved_y))
    only_x = jnp.logical_and(moved_x, jnp.logical_not(moved_y))
    only_y = jnp.logical_and(moved_y, jnp.logical_not(moved_x))
    use_land = either(
        only_x, either(jnp.logical_and(row2, only_y), jnp.logical_and(row3, both))
    )
    use_sib1 = jnp.logical_and(either(row1, row3), only_y)
    use_sib2 = jnp.logical_and(either(row1, row2), both)

    def choose(z):
        value = jnp.where(use_sib2, sib2[z], jnp.zeros((SIDE, SIDE), BF16))
        value = jnp.where(use_sib1, sib1[z], value)
        value = jnp.where(use_land, land[z], value)
        return jnp.where(use_own, own[z], value)

    def forward(k, h):
        piece = part(k, h)

        @pl.when(has_prev)
        def _():
            h1(piece).wait_recv()

        @pl.when(row0)
        def _():
            s1(piece).wait_recv()
            blend(sib1, relay, piece[0])
            h2(stage, piece).start()

        @pl.when(jnp.logical_not(row0))
        def _():
            h2(relay, piece).start()

        @pl.when(row3)
        def _():
            s2(relay, piece).start()

        if isinstance(k, int) and k >= 6:
            send(part(*{(7, 0): (6, 1), (6, 0): (5, 0), (7, 1): (5, 1), (6, 1): (4, 0)}[k, h]))
        else:
            @pl.when(k >= 1 + h)
            def _():
                send(part(k - 1 - h, 1 - h))

    def landing(piece):
        h2(relay, piece).wait_recv()

        @pl.when(row0)
        def _():
            s2(land, piece).start()

        @pl.when(row1)
        def _():
            s1(piece).wait_recv()

        @pl.when(either(row1, row2))
        def _():
            s2(relay, piece).wait_recv()

    up_z = remote(top_out, top_in, fine_s.at[0], fine_r.at[0], high_slab)

    @pl.when(row0)
    def _():
        flag_up.wait_recv()

    forward(7, 0)

    rhs_lane = iota((2 * SIDE, 2 * SIDE), 1)
    rhs_row = iota((2 * SIDE, 2 * SIDE), 0)
    col = lax.rem(rhs_lane, SIDE)
    is_lerp = rhs_lane < SIDE
    here = jnp.where(is_lerp, 1.0 - tx, -1.0)
    there = jnp.where(is_lerp, tx, 1.0)
    top = jnp.where(rhs_row == col, here, jnp.where(rhs_row == col + 1, there, 0.0))
    rhs[...] = jnp.where(
        rhs_row < SIDE, top, jnp.where(col == SIDE - 1, there, 0.0)
    ).astype(BF16)

    point = lax.rem(lane, 32) - 8
    tap = lane // 32
    px_ok = jnp.logical_and(g * 16 + point >= 0, g * 16 + point < 16 * GX)
    basis_x = jnp.where(px_ok, spline(row.astype(F32) / S - point.astype(F32)), 0.0)
    for m in range(4):
        scale = jnp.full((SIDE, SIDE), float(TAPS[m, 3]), F32)
        for a in (2, 1, 0):
            scale = jnp.where(tap == a, float(TAPS[m, a]), scale)
        high, low = split(basis_x * scale)
        for half in range(2):
            rhs_x[pl.ds(m * 256 + half * 128, 128), pl.ds(0, 128)] = high
            rhs_x[pl.ds(m * 256 + half * 128, 128), pl.ds(128, 128)] = low

    q_point = iota((32, SIDE), 0) - 8
    q_ok = jnp.logical_and(r * 16 + q_point >= 0, r * 16 + q_point < 16 * GY)
    basis_y = jnp.where(
        q_ok, spline(iota((32, SIDE), 1).astype(F32) / S - q_point.astype(F32)), 0.0
    ) * (live * S ** (-1.5))
    high, low = split(basis_y)
    lhs_y[pl.ds(0, 32), pl.ds(0, 128)] = high
    lhs_y[pl.ds(0, 32), pl.ds(128, 128)] = high
    lhs_y[pl.ds(32, 32), pl.ds(0, 128)] = low
    lhs_y[pl.ds(32, 32), pl.ds(128, 128)] = jnp.zeros((32, SIDE), BF16)

    coarse_y = mm_full(weight(iota((16, 32), 1) - 8 - 2 * (iota((16, 32), 0) - 1)), basis_y)
    high, low = split(coarse_y)
    lhs_y[pl.ds(64, 16), pl.ds(0, 128)] = high
    lhs_y[pl.ds(64, 16), pl.ds(128, 128)] = high
    lhs_y[pl.ds(80, 16), pl.ds(0, 128)] = low
    lhs_y[pl.ds(80, 16), pl.ds(128, 128)] = jnp.zeros((16, SIDE), BF16)

    def cell_weights(k, carry):
        z_point = k + row // 32 - 1
        z_ok = jnp.logical_and(l * 8 + z_point >= 0, l * 8 + z_point < 8 * GZ)
        both_w = weight(z_point - 2 * (lane // 16 - 1)) * weight(
            lax.rem(row, 32) - 8 - 2 * (lax.rem(lane, 16) - 1)
        )
        w_c[k] = jnp.where(z_ok, both_w, 0.0).astype(BF16)
        return carry

    lax.fori_loop(0, CELLS, cell_weights, 0)
    coarse[...] = jnp.zeros((48, SIDE), F32)
    wr, wl = iota((512, SIDE), 0), iota((512, SIDE), 1)

    forward(6, 0)

    def arrive(copy, dst, ok):
        @pl.when(ok)
        def _():
            copy.wait_recv()

        @pl.when(jnp.logical_not(ok))
        def _():
            dst[...] = jnp.zeros(dst.shape, BF16)

    arrive(s_right, e_x.at[rows_s], has_prev)
    arrive(t_left, e_x.at[rows_t], has_next)

    @pl.when(has_low)
    def _():
        x_low.start()

    @pl.when(has_high)
    def _():
        x_high.start()

    kz = 4 * (iota((512, 16), 0) // 128) + lax.rem(iota((512, 16), 0) // 16, 8) - 1
    pick_z = (kz == iota((512, 16), 1)).astype(F32)
    spread_z = weight(l * 8 + iota((16, SIDE), 1) // 16 - 2 * iota((16, SIDE), 0))
    full_z = mm_full(mm_full(pick_z, pz[...], ((1,), (1,))), spread_z)
    full_z = jnp.where(lax.rem(wr, 16) == lax.rem(wl, 16), full_z, 0.0)
    high, low = split(full_z)
    w_z[0], w_z[1] = high, low

    jy = 8 * (iota((32, 64), 1) // 16) + lax.rem(iota((32, 64), 1), 16) - 1
    pick_y = (jy == iota((32, 64), 0)).astype(F32)
    spread_y = weight(r * 16 + iota((16, 32), 0) - 2 * iota((16, 32), 1))
    full_y = mm_full(spread_y, mm_full(py[...], pick_y))
    high, low = split(full_y)
    m_y[...] = jnp.concatenate(
        [
            jnp.concatenate([high.astype(F32), high.astype(F32)], axis=1),
            jnp.concatenate([low.astype(F32), jnp.zeros((16, 64), F32)], axis=1),
        ],
        axis=0,
    ).astype(BF16)

    xl = iota((64, 512), 1)
    spread_x = weight(16 * (2 * (xl // 128) + lax.rem(g, 2)) + lax.rem(xl, 16) - 2 * iota((64, 512), 0))
    kx = 8 * (g - lax.rem(g, 2) + iota((256, 64), 0) // 128) + lax.rem(iota((256, 64), 0), 16) - 1
    pick_x = (kx == iota((256, 64), 1)).astype(F32)
    full_x = mm_full(pick_x, mm_full(px[...], spread_x, ((0,), (0,))))
    same = lax.rem(iota((256, 512), 0) // 16, 8) == lax.rem(iota((256, 512), 1) // 16, 8)
    high, low = split(jnp.where(same, full_x, 0.0))
    w_x[0], w_x[1] = high, low

    def clear_acc(i, carry):
        acc[i] = jnp.zeros((32, 384), F32)
        return carry

    lax.fori_loop(0, 4, clear_acc, 0)

    arrive(own_low, e_up, has_high)
    arrive(own_high, e_down, has_low)
    arrive(x_low, e_up_x, has_high)
    arrive(x_high, e_down_x, has_low)

    def pick(stay, by_x, by_y, by_both):
        return jnp.where(moved_y, jnp.where(moved_x, by_both, by_y), jnp.where(moved_x, by_x, stay))

    def wide(ref, rows):
        return ref[rows, :].astype(F32)

    t_here, t_right = wide(e_own, rows_t), wide(e_x, rows_t)
    t_wide = pick(t_right, t_here, e_down_x[...].astype(F32), e_down[...].astype(F32))
    t_sel[...] = jnp.transpose(jnp.concatenate([t_wide, jnp.zeros((48, SIDE), F32)], axis=0))
    s_sel = pick(wide(e_up, rows_s), wide(e_up_x, rows_s), wide(e_own, rows_s), wide(e_x, rows_s))
    k_sel = pick(wide(e_up_x, rows_t), wide(e_up, rows_t), t_right, t_here)
    diag = jnp.where(lane[:80] == row[:80], jnp.broadcast_to(k_sel[:, 0:1], (80, SIDE)), 0.0)
    bottom = mm(jnp.concatenate([s_sel, diag], axis=1).astype(BF16), rhs[...])
    a_bot[...] = bottom[:, :SIDE]
    b_bot[...] = bottom[:, SIDE:]

    load_fixed.wait()

    def fill(z, j):
        lhs[pl.ds(j * SIDE, SIDE), pl.ds(0, SIDE)] = choose(z)
        lhs[pl.ds(j * SIDE, SIDE), pl.ds(SIDE, SIDE)] = jnp.where(lane == z, t_sel[...], 0.0).astype(BF16)

    def lerp_x(z, slot, count):
        for j in range(count):
            fill(z + j, j)
        both_x = mm(lhs[pl.ds(0, count * SIDE), :], rhs[...])
        for j in range(count):
            rows = slice(j * SIDE, (j + 1) * SIDE)
            a_buf[slot + j, pl.ds(0, SIDE), :] = both_x[rows, :SIDE]
            b_buf[slot + j, pl.ds(0, SIDE), :] = both_x[rows, SIDE:]
            a_buf[slot + j, pl.ds(SIDE, 1), :] = a_bot[pl.ds(z + j, 1), :]
            b_buf[slot + j, pl.ds(SIDE, 1), :] = b_bot[pl.ds(z + j, 1), :]

    def rows_of(j, y0):
        a = a_buf[j, pl.ds(y0, 16), :]
        b = b_buf[j, pl.ds(y0, 16), :]
        dy = a_buf[j, pl.ds(y0 + 1, 16), :] - a
        along_xy = a + ty * dy
        diff_xy = b + ty * (b_buf[j, pl.ds(y0 + 1, 16), :] - b)
        return along_xy, diff_xy, dy

    def compute(k):
        def tile(t, carry):
            y0 = pl.multiple_of(t * 16, 16)
            w1, x1, y1 = rows_of(S, y0)
            sums = [[jnp.zeros((16, SIDE), F32) for _ in range(4)] for _ in range(3)]
            for j in reversed(range(S)):
                w0, x0, yy0 = rows_of(j, y0)
                gz = w1 - w0
                res = w0 + tz * gz - fixed[k * S + j, pl.ds(y0, 16), :].astype(F32)
                grads = (x0 + tz * (x1 - x0), yy0 + tz * (y1 - yy0), gz)
                for d in range(3):
                    value = res * grads[d]
                    for m in range(4):
                        value = sums[d][m] + value
                        sums[d][m] = value
                w1, x1, y1 = w0, x0, yy0
            for d in range(3):
                for m in range(4):
                    high, low = split(sums[d][m])
                    place = pl.ds(pl.multiple_of(d * SIDE + y0, 16), 16)
                    mom[place, pl.ds(m * 256, 128)] = high
                    mom[place, pl.ds(m * 256 + 128, 128)] = low
            return carry

        lax.fori_loop(0, SIDE // 16, tile, 0)
        a_buf[S] = a_buf[0]
        b_buf[S] = b_buf[0]

        parts = mm(mom[...], rhs_x[...])
        parts = parts[:, :SIDE] + parts[:, SIDE:]
        wide = jnp.concatenate([parts[d * SIDE:(d + 1) * SIDE] for d in range(3)], axis=1)
        high, low = split(wide)
        h_x[pl.ds(0, SIDE), :] = high
        h_x[pl.ds(SIDE, SIDE), :] = low
        both_y = mm(lhs_y[...], h_x[...])
        rough = both_y[64:80] + both_y[80:96]
        rough = jnp.concatenate([rough[:, d * SIDE:(d + 1) * SIDE] for d in range(3)], axis=0)
        high, low = split(rough)
        weights = w_c[k]
        coarse[...] += mm(high, weights) + mm(low, weights)
        done = both_y[:32] + both_y[32:64]
        turn = lax.rem(k + 3, 4)
        base = (k + 3) // 4
        blocks = iota((32, SIDE), 1) // 32
        for d in range(3):
            moved = pltpu.roll(done[:, d * SIDE:(d + 1) * SIDE], turn * 32, 1)
            place = pl.ds(d * SIDE, SIDE)
            acc[base, :, place] += jnp.where(blocks >= turn, moved, 0.0)
            acc[base + 1, :, place] += jnp.where(blocks < turn, moved, 0.0)

    def land_half(k, h):
        piece = part(k, h)
        landing(piece)
        lerp_x(k * S + h * HALF, h * HALF, piece[0].size)

    def more(k):
        @pl.when(jnp.logical_not(row3))
        def _():
            for h in (0, 1):
                s1(part(k, h)).start()

    more(4)
    forward(7, 1)
    land_half(7, 0)
    forward(6, 1)
    land_half(7, 1)
    compute(7)

    def step(n, carry):
        k = 6 - n

        @pl.when(k >= 3)
        def _():
            more(k - 3)

        for h in (0, 1):
            @pl.when(k >= 1)
            def _(h=h):
                forward(k - 1, h)

            land_half(k, h)
        compute(k)

        @pl.when(k == 6)
        def _():
            top_out[...] = acc[3]

            @pl.when(above)
            def _():
                up_z.start()

        return carry

    lax.fori_loop(0, CELLS - 1, step, 0)

    c_z[l] = coarse[...]
    z_turns = (2, 1, 3)
    z_copies = [
        remote(c_z.at[l], c_z.at[l], cz_s.at[o], cz_r.at[l], (g, r, lax.rem(l + o, GZ))) for o in z_turns
    ]
    for copy in z_copies:
        copy.start()

    def drain(piece):
        h2(relay, piece).wait_send()

        @pl.when(jnp.logical_not(row3))
        def _():
            s1(piece).wait_send()

        @pl.when(has_next)
        def _():
            h1(piece).wait_send()

        @pl.when(either(row0, row3))
        def _():
            s2(relay, piece).wait_send()

    def drain_cell(k, carry):
        for h in (0, 1):
            drain(part(k, h))
        return carry

    lax.fori_loop(0, CELLS - 1, drain_cell, 0)
    drain_cell(CELLS - 1, 0)

    blocks = iota((32, SIDE), 1) // 32
    packed = jnp.zeros((32, SIDE), F32)
    for d in range(3):
        packed += jnp.where(
            blocks == d, pltpu.roll(acc[0, :, pl.ds(d * SIDE, SIDE)], 32 * (d + 1), 1), 0.0
        )
    low_out[...] = packed
    down_z = remote(low_out, low_in, fine_s.at[1], fine_r.at[1], low_slab)

    @pl.when(below)
    def _():
        down_z.start()

    fold[...] = acc[pl.ds(1, 2)]

    def weigh(block, weights, at):
        high, low = split(block)
        rows = block.shape[0]
        pair = mm(jnp.concatenate([high, low], axis=0), weights[0, at, :])
        return pair[:rows] + pair[rows:] + mm(high, weights[1, at, :])

    def span(dev):
        return pl.ds(pl.multiple_of(dev * SIDE, SIDE), SIDE)

    total = weigh(coarse[...], w_z, span(l))
    for o in (1, 3, 2):
        dev = lax.rem(l + o, GZ)
        remote(c_z.at[dev], c_z.at[dev], cz_s.at[o], cz_r.at[dev], partner).wait_recv()
        total += weigh(c_z[dev], w_z, span(dev))
    slot = GY * lax.rem(g, 2) + r
    c_y[slot] = total
    y_turns = [(1, 2), (1, 1), (1, 3), (1, 0), (0, 2), (0, 1), (0, 3)]
    y_copies = [
        remote(
            c_y.at[slot], c_y.at[slot], cy_s.at[i], cy_r.at[slot],
            (mate if dx else g, lax.rem(r + o, GY), l),
        )
        for i, (dx, o) in enumerate(y_turns)
    ]
    for copy in y_copies:
        copy.start()

    @pl.when(below)
    def _():
        up_z.wait_recv()
        fold[0] += top_in[...]

    @pl.when(above)
    def _():
        down_z.wait_recv()
        for d in range(3):
            turned = pltpu.roll(low_in[...], SIDE - 32 * (d + 1), 1)
            fold[1, :, pl.ds(d * SIDE, SIDE)] += jnp.where(blocks == 3, turned, 0.0)

    up_y = remote(fold.at[:, pl.ds(24, 8)], f_y.at[0], fine_s.at[2], fine_r.at[2], high_row)
    down_y = remote(fold.at[:, pl.ds(0, 8)], f_y.at[1], fine_s.at[3], fine_r.at[3], low_row)

    @pl.when(has_high)
    def _():
        up_y.start()

    @pl.when(has_low)
    def _():
        down_y.start()

    for i, (dx, o) in reversed(list(enumerate(y_turns))):
        dev = GY * lax.rem(g + dx, 2) + lax.rem(r + o, GY)
        remote(c_y.at[dev], c_y.at[dev], cy_s.at[i], cy_r.at[dev], partner).wait_recv()
    gathered = jnp.concatenate(
        [
            jnp.concatenate(
                [c_y[GY * dx + row, pl.ds(d * 16, 16), :] for dx in range(2) for d in range(3)], axis=1
            )
            for row in range(GY)
        ],
        axis=0,
    )
    high, low = split(gathered)
    both_y = mm(m_y[...], jnp.concatenate([high, low], axis=0))
    both_y = both_y[:16] + both_y[16:]
    both_y = jnp.concatenate(
        [
            jnp.concatenate(
                [both_y[:, (dx * 3 + d) * SIDE:(dx * 3 + d + 1) * SIDE] for dx in range(2)], axis=1
            )
            for d in range(3)
        ],
        axis=0,
    )
    corr = weigh(both_y, w_x, slice(None))
    for t in range(GZ):
        c_out[t] = corr[:, t * SIDE:(t + 1) * SIDE]

    z_own = g // 2
    x_copies = [
        remote(
            c_out.at[lax.rem(z_own + o, 4)], c_x.at[z_own], cx_s.at[o], cx_r.at[z_own],
            (lax.rem(g + 2 * o, GX), r, l),
        )
        for o in (2, 1, 3)
    ]
    for copy in x_copies:
        copy.start()

    @pl.when(has_low)
    def _():
        up_y.wait_recv()
        fold[:, pl.ds(8, 8), :] += f_y[0]

    @pl.when(has_high)
    def _():
        down_y.wait_recv()
        fold[:, pl.ds(16, 8), :] += f_y[1]

    spot = lax.rem(iota((16, SIDE), 1), 32)
    parts = [
        fold[half, pl.ds(8, 16), pl.ds(d * SIDE, SIDE)] for half in range(2) for d in range(3)
    ]
    to_right, to_left = jnp.zeros((16, SIDE), F32), jnp.zeros((16, SIDE), F32)
    for n, value in enumerate(parts):
        ends = jnp.where(jnp.logical_or(spot == 24, spot == 25), value, 0.0)
        to_right += ends if n == 0 else pltpu.roll(ends, 2 * n, 1)
        ends = jnp.where(spot == 7, value, 0.0)
        to_left += ends if n == 0 else pltpu.roll(ends, n, 1)
    x_out[0] = to_right
    x_out[1] = to_left
    up_x = remote(x_out.at[0], x_in.at[0], fine_s.at[4], fine_r.at[4], right)
    down_x = remote(x_out.at[1], x_in.at[1], fine_s.at[5], fine_r.at[5], left)

    @pl.when(has_next)
    def _():
        up_x.start()

    @pl.when(has_prev)
    def _():
        down_x.start()

    @pl.when(jnp.logical_not(has_prev))
    def _():
        x_in[0] = jnp.zeros((16, SIDE), F32)

    @pl.when(jnp.logical_not(has_next))
    def _():
        x_in[1] = jnp.zeros((16, SIDE), F32)

    corr = c_out[z_own]

    def take(o):
        dev = lax.rem(z_own + o, 4)
        remote(c_x.at[dev], c_x.at[dev], cx_s.at[o], cx_r.at[dev], partner).wait_recv()
        return c_x[dev]

    @pl.when(has_prev)
    def _():
        up_x.wait_recv()

    @pl.when(has_next)
    def _():
        down_x.wait_recv()

    from_left, from_right = x_in[0], x_in[1]
    fine = []
    for n, value in enumerate(parts):
        before = pltpu.roll(from_left, SIDE - 16 - 2 * n, 1)
        after = pltpu.roll(from_right, 16 - n, 1)
        value = value + jnp.where(jnp.logical_or(spot == 8, spot == 9), before, 0.0)
        fine.append(value + jnp.where(spot == 23, after, 0.0))

    for o in (1, 3, 2):
        corr += take(o)
    for half in range(2):
        for d in range(3):
            value = fine[half * 3 + d]
            for b in range(4):
                at = (half * 4 + b) * 16
                out[d, half * 4 + b] = (
                    value[:, b * 32 + 8:b * 32 + 24] + corr[d * 16:(d + 1) * 16, at:at + 16]
                )

    @pl.when(below)
    def _():
        plane.wait_send()
        down_z.wait_send()

    @pl.when(above)
    def _():
        up_z.wait_send()

    @pl.when(has_low)
    def _():
        own_low.wait_send()
        x_low.wait_send()
        down_y.wait_send()

    @pl.when(has_high)
    def _():
        own_high.wait_send()
        x_high.wait_send()
        up_y.wait_send()

    @pl.when(has_prev)
    def _():
        t_left.wait_send()
        down_x.wait_send()

    @pl.when(has_next)
    def _():
        s_right.wait_send()
        up_x.wait_send()

    @pl.when(row2)
    def _():
        flag_up.wait_send()

    @pl.when(asks_left)
    def _():
        flag_left.wait_send()

    for copy in z_copies + y_copies + x_copies:
        copy.wait_send()


def per_device(
    fixed_image, moving_image, block_shift, fraction, brick_valid, precond_x, precond_y, precond_z
):
    dma = pltpu.SemaphoreType.DMA
    vmem = pltpu.VMEM
    brick = vmem((DEPTH + 1, SIDE, SIDE), BF16)
    hbm_spec = pl.BlockSpec(memory_space=pltpu.HBM)
    smem = pltpu.SMEM
    vmem_spec = pl.BlockSpec(memory_space=pltpu.VMEM)
    return pl.pallas_call(
        kernel,
        out_shape=jax.ShapeDtypeStruct((3, 8, 16, 16), F32),
        in_specs=[hbm_spec] * 8,
        out_specs=vmem_spec,
        scratch_shapes=[
            smem((2,), jnp.int32), smem((3,), jnp.int32), smem((1, 1, 1), jnp.int32),
            vmem((64, 64), F32), vmem((32, 32), F32), vmem((16, 16), F32),
            brick, brick, brick, brick, brick, brick,
            vmem((DEPTH, SIDE, SIDE), BF16),
            vmem((8, SIDE), F32), vmem((8, SIDE), F32),
            vmem((160, SIDE), BF16), vmem((160, SIDE), BF16), vmem((160, SIDE), BF16),
            vmem((160, SIDE), BF16), vmem((80, SIDE), BF16), vmem((80, SIDE), BF16),
            vmem((SIDE, SIDE), F32), vmem((80, SIDE), F32), vmem((80, SIDE), F32),
            vmem((S * SIDE, 256), BF16), vmem((256, 256), BF16),
            vmem((S + 1, SIDE + 8, SIDE), F32), vmem((S + 1, SIDE + 8, SIDE), F32),
            vmem((3 * SIDE, 1024), BF16), vmem((1024, 256), BF16), vmem((96, 256), BF16),
            vmem((4, 32, 384), F32), vmem((48, SIDE), F32), vmem((CELLS, SIDE, SIDE), BF16),
            vmem((2, 512, SIDE), BF16), vmem((2, 256, 512), BF16), vmem((32, SIDE), BF16),
            vmem((GZ, 48, SIDE), F32), vmem((8, 48, SIDE), F32), vmem((4, 48, SIDE), F32), vmem((4, 48, SIDE), F32),
            vmem((32, 384), F32), vmem((32, 384), F32), vmem((32, SIDE), F32), vmem((32, SIDE), F32),
            vmem((2, 2, 8, 384), F32), vmem((2, 16, SIDE), F32), vmem((2, 16, SIDE), F32),
            vmem((2, 32, 384), F32), vmem((256, 384), BF16),
            dma((8,)),
            *[dma((PIECES,))] * 8,
            dma((8,)), dma((8,)), dma((6,)), dma((6,)),
            dma((GZ,)), dma((GZ,)), dma((8,)), dma((8,)), dma((4,)), dma((4,)),
        ],
        compiler_params=pltpu.CompilerParams(
            collective_id=0, has_side_effects=True, vmem_limit_bytes=53 * 2**20
        ),
        name="registration_gradient",
    )(
        *(
            pltpu.with_memory_space_constraint(x, pltpu.HBM)
            for x in (
                moving_image, fixed_image, block_shift.reshape(2), fraction.reshape(3)
            )
        ),
        brick_valid,
        *(pltpu.with_memory_space_constraint(x, pltpu.HBM) for x in (precond_x, precond_y, precond_z)),
    )


def solution(mesh):
    return jax.shard_map(
        per_device,
        mesh=mesh,
        in_specs=(
            P("gz", "gy", "gx"),
            P("gz", "gy", "gx"),
            P(None, "gz", "gy", "gx"),
            P(None, "gz", "gy", "gx"),
            P("gz", "gy", "gx"),
            P(),
            P(),
            P(),
        ),
        out_specs=P(None, "gz", "gy", "gx"),
        check_vma=False,
    )
```
